256 devices in a mesh: dp: 16 (over x, z_lo, core), tensor: 16 (over y, z_hi).
Axes of the slice: x: 4, y: 4, z: 8 (z_hi: 4, z_lo: 2; z = z_hi * 2 + z_lo), core: 2. Of those that a mesh axis runs over, the one named last changes fastest.
Arguments:
- gate_pre: bfloat16 [2048, 28672], P('dp', 'tensor'), may hold values from -6 to 6
- up_pre: bfloat16 [2048, 28672], P('dp', 'tensor'), may hold values from -6 to 6
- down_rotated: bfloat16 [28672, 8192], P('tensor', 'dp'), may hold values from -0.03125 to 0.03125
- exponents: int32 [224, 8192], P('tensor', 'dp'), may hold values from -10 to -7
- signs: int32 [28672], P('tensor'), may hold values from 0 to 1
- out_grad: bfloat16 [2048, 8192], P('tensor', 'dp'), may hold values from -6 to 6
Outputs:
- layer_out: bfloat16 [2048, 8192], P('tensor', 'dp')
- grad_down: float32 [28672, 8192], P('tensor', 'dp')
- grad_gate: bfloat16 [2048, 28672], P('dp', 'tensor')
- grad_up: bfloat16 [2048, 28672], P('dp', 'tensor')
The draws below stay inside these ranges and needn't reach their ends.
All inputs are finite; a program needn't handle non-finite values.
Results may differ from the reference program's by a relative error of at most 0.025.
Values may be sent and summed in bfloat16 or wider, within the bound.
A program may use at most 128 MiB of HBM per device.

```python
import jax
import jax.numpy as jnp
import numpy as np
from jax import lax

D = 8192
FF = 28672
WALSH = 128
GROUP = 128
TOKENS = 2048
COS = 14
N_DP = 16
N_TENSOR = 16


def set_ends(drawn, stream_key, smallest, top_value):
    dims = drawn.shape
    place = [jax.random.randint(jax.random.fold_in(stream_key, axis), (), 0, dims[axis]) for axis in range(len(dims))]
    drawn = drawn.at[tuple(place)].set(smallest)
    longest = dims.index(max(dims))
    place[longest] = (place[longest] + 1) % dims[longest]
    return drawn.at[tuple(place)].set(top_value)


def level_of(own_key, dims, pieces, low, top_value):
    loudness = 1.0
    for dim, shards_of in pieces:
        draws = jax.random.uniform(jax.random.fold_in(jax.random.fold_in(own_key, 6), dim), (shards_of,), jnp.float32, low / len(pieces), top_value / len(pieces))
        loudness = loudness * jnp.repeat(jnp.exp(draws), dims[dim] // shards_of).reshape((-1,) + (1,) * (len(dims) - 1 - dim))
    return loudness


def gaussian(key, extent, scale, reach, split=(), kind=jnp.bfloat16):
    array = scale * jax.random.normal(key, extent, jnp.float32)
    if split:
        array = array * level_of(key, extent, split, -0.22, 0.18)
    return jnp.clip(array, -reach, reach).astype(kind)


def setup_inputs(seed: int = 0) -> dict:
    splits = jax.random.split(jax.random.key(seed), 7)
    return {
        "gate_pre": gaussian(splits[0], (TOKENS, FF), 1.0, 6.0, ((0, 16), (1, 16))),
        "up_pre": gaussian(splits[1], (TOKENS, FF), 1.0, 6.0, ((0, 16), (1, 16))),
        "down_rotated": gaussian(splits[2], (FF, D), FF ** -0.5, 0.03125, ((0, 16), (1, 16))),
        "exponents": set_ends(jax.random.randint(splits[3], (FF // GROUP, D), -10, -6), jax.random.fold_in(splits[3], 1), -10, (-6) - 1).astype(jnp.int32),
        "signs": set_ends(jax.random.randint(splits[4], (FF,), 0, 2), jax.random.fold_in(splits[4], 1), 0, 1).astype(jnp.int32),
        "out_grad": gaussian(splits[5], (TOKENS, D), 1.0, 6.0, ((0, 16), (1, 16))),
    }


HIGH = lax.Precision.HIGHEST

def sylvester(order):
    left = np.arange(order)[:, None]
    right = np.arange(order)[None, :]
    anded = left & right
    parity = np.zeros((order, order), np.int64)
    for bit in range(max(order.bit_length(), 1)):
        parity = parity + (anded >> bit & 1)
    table = 1.0 - 2.0 * (parity % 2)
    return jnp.asarray(table / np.sqrt(order), jnp.float32)

def cosine(order):
    rows = np.arange(order)[:, None]
    cols = np.arange(order)[None, :]
    table = np.sqrt(2.0 / order) * np.cos(np.pi * (2 * rows + 1) * cols / (2.0 * order))
    table = np.where(cols == 0, np.sqrt(1.0 / order), table)
    return jnp.asarray(table, jnp.float32)

def reference(gate_pre, up_pre, down_rotated, exponents, signs, out_grad):
    walsh = sylvester(WALSH)
    cos_table = cosine(COS)
    cross = sylvester(N_TENSOR)
    gate = gate_pre.astype(jnp.float32)
    up = up_pre.astype(jnp.float32)
    active = jax.nn.silu(gate)
    hidden = (active * up).astype(jnp.bfloat16)
    sign_f = (2 * signs - 1).astype(jnp.float32)
    shaped = (hidden.astype(jnp.float32) * sign_f).reshape(TOKENS, N_TENSOR, COS, WALSH)
    shaped = jnp.einsum('atmk,kl->atml', shaped, walsh, precision=HIGH)
    shaped = jnp.einsum('atmk,mn->atnk', shaped, cos_table, precision=HIGH)
    shaped = jnp.einsum('atmk,tu->aumk', shaped, cross, precision=HIGH)
    rotated = shaped.reshape(TOKENS, FF).astype(jnp.bfloat16)
    scale = jnp.repeat(jnp.exp2(exponents.astype(jnp.float32)), GROUP, axis=0)
    squash = jnp.tanh(down_rotated.astype(jnp.float32) / (7.0 * scale))
    weight_q = (7.0 * scale * squash).astype(jnp.bfloat16)
    layer_out = jnp.dot(rotated, weight_q, preferred_element_type=jnp.float32).astype(jnp.bfloat16)
    grad_w = lax.dot_general(rotated, out_grad, (((0,), (0,)), ((), ())), preferred_element_type=jnp.float32)
    grad_down = grad_w * (1.0 - squash * squash)
    width = D // N_DP
    grad_rot = jnp.zeros((TOKENS, FF), jnp.float32)
    for block in range(N_DP):
        part = lax.dot_general(out_grad[:, block * width:(block + 1) * width], weight_q[:, block * width:(block + 1) * width], (((1,), (1,)), ((), ())), preferred_element_type=jnp.float32)
        part = lax.optimization_barrier(part.astype(jnp.bfloat16))
        grad_rot = grad_rot + part.astype(jnp.float32)
    shaped = grad_rot.reshape(TOKENS, N_TENSOR, COS, WALSH)
    shaped = jnp.einsum('atmk,tu->aumk', shaped, cross, precision=HIGH)
    shaped = jnp.einsum('atnk,mn->atmk', shaped, cos_table, precision=HIGH)
    shaped = jnp.einsum('atmk,kl->atml', shaped, walsh, precision=HIGH)
    grad_hidden = shaped.reshape(TOKENS, FF) * sign_f
    sigma = jax.nn.sigmoid(gate)
    grad_gate = (grad_hidden * up * sigma * (1.0 + gate * (1.0 - sigma))).astype(jnp.bfloat16)
    grad_up = (grad_hidden * active).astype(jnp.bfloat16)
    return (layer_out, grad_down, grad_gate, grad_up)
```

```python
import jax
import jax.numpy as jnp
import ml_dtypes
import numpy as np
from jax import lax
from jax.experimental import pallas as pl
from jax.experimental.pallas import tpu as pltpu
from jax.sharding import PartitionSpec as P

ROWS = 128
WIDTH = 1792
FEAT = 512
WALSH = 128
COS = 14
HALF = 896
F32 = jnp.float32
BF16 = jnp.bfloat16
MESH = pl.DeviceIdType.MESH

COSINE = np.sqrt(2.0 / COS) * np.cos(
    np.pi * (2 * np.arange(COS)[:, None] + 1) * np.arange(COS)[None, :] / (2.0 * COS)
)
COSINE[:, 0] = np.sqrt(1.0 / COS)
COSINE = COSINE / np.sqrt(WALSH)


def walsh_signs(order):
    a = np.arange(order)[:, None] & np.arange(order)[None, :]
    parity = np.zeros((order, order), np.int64)
    for bit in range(order.bit_length()):
        parity = parity + (a >> bit & 1)
    return (1.0 - 2.0 * (parity % 2)).astype(ml_dtypes.bfloat16)


def walsh_16(src, dst):
    @pl.loop(0, HALF // 128)
    def _(ch):
        cols = pl.ds(pl.multiple_of(ch * 128, 128), 128)
        v = [src[k, :, cols].astype(F32) for k in range(16)]
        for bit in range(4):
            step = 1 << bit
            w = list(v)
            for k in range(16):
                if not k & step:
                    w[k] = v[k] + v[k + step]
                    w[k + step] = v[k] - v[k + step]
            v = w
        for k in range(16):
            dst[k, :, cols] = (v[k] * 0.25).astype(BF16)


def nt(a, b):
    return lax.dot_general(a, b, (((1,), (1,)), ((), ())), preferred_element_type=F32)


def tn(a, b):
    return lax.dot_general(a, b, (((0,), (0,)), ((), ())), preferred_element_type=F32)


def kernel(
    gate, up, w, ex, sg, g, hw,
    lo_out, gd_out, gg_out, gu_out,
    hs, r1, s2, r2, hb, r3, s4, r4, uu,
    gall, wq, dsq, rot,
    pbuf, rsa, rsb, zsnd, zrcv,
    lo, ta, tb, lz, tc, td,
    a_s, a_r, g_s, g_r, c_s, c_r, p_s, p_r, k_s, k_r, t_s, t_r,
):
    dp = lax.axis_index("dp")
    t = lax.axis_index("tensor")
    x, zl, c = dp // 4, (dp // 2) % 2, dp % 2
    y, zh = t // 4, t % 4
    xp, xm, xo = (x + 1) % 4, (x + 3) % 4, (x + 2) % 4
    yp, ym, yo = (y + 1) % 4, (y + 3) % 4, (y + 2) % 4
    hp, hm, ho = (zh + 1) % 4, (zh + 3) % 4, (zh + 2) % 4
    zo, co = 1 - zl, 1 - c
    to_xp = (xp * 4 + zl * 2 + c, t)
    to_xm = (xm * 4 + zl * 2 + c, t)
    to_zl = (x * 4 + zo * 2 + c, t)
    to_co = (x * 4 + zl * 2 + co, t)
    to_yp, to_ym = (dp, yp * 4 + zh), (dp, ym * 4 + zh)
    to_hp, to_hm = (dp, y * 4 + hp), (dp, y * 4 + hm)

    def copy(src, dst, ss, rs, dev):
        return pltpu.make_async_remote_copy(
            src_ref=src, dst_ref=dst, send_sem=ss, recv_sem=rs, device_id=dev, device_id_type=MESH
        )

    sent = []

    def send(src, dst, ss, rs, dev):
        d = copy(src, dst, ss, rs, dev)
        d.start()
        sent.append(d)

    def arrived(dst, ss, rs, dev):
        copy(dst, dst, ss, rs, dev).wait_recv()

    barrier = pltpu.get_barrier_semaphore()

    @pl.loop(1, 16)
    def _(j):
        pl.semaphore_signal(barrier, inc=1, device_id=(dp, (t + j) % 16), device_id_type=MESH)

    for dev in (to_xp, to_xm, to_zl, to_co):
        pl.semaphore_signal(barrier, inc=1, device_id=dev, device_id_type=MESH)

    sign = 2.0 * sg[...].astype(F32) - 1.0

    @pl.loop(0, 8)
    def _(i):
        rows = pl.ds(pl.multiple_of(i * 16, 16), 16)
        v = gate[rows, :].astype(F32)
        h = (v * jax.nn.sigmoid(v) * up[rows, :].astype(F32)).astype(BF16).astype(F32)
        h = (h * sign).astype(BF16)
        hs[2 * i] = h[:, :HALF]
        hs[2 * i + 1] = h[:, HALF:]

    pl.semaphore_wait(barrier, 19)

    def gblk(core, yy, hh):
        return gall.at[core, hh % 2, yy * 2 + hh // 2]

    def ghalf(core, yy, hh, top):
        return gall.at[core, hh % 2, yy * 2 + hh // 2, pl.ds(0 if top else 64, 64)]

    zs = (zh, hm, hp, ho)

    def g_y1(j):
        b = gblk(c, y, zs[j])
        send(b, b, g_s.at[4 + 2 * j], g_r.at[4 + 2 * j], to_yp)
        send(b, b, g_s.at[5 + 2 * j], g_r.at[5 + 2 * j], to_ym)

    def g_y2(j):
        arrived(gblk(c, ym, zs[j]), g_s.at[4 + 2 * j], g_r.at[4 + 2 * j], to_ym)
        b = ghalf(c, ym, zs[j], True)
        send(b, b, g_s.at[12 + 2 * j], g_r.at[12 + 2 * j], to_yp)
        arrived(gblk(c, yp, zs[j]), g_s.at[5 + 2 * j], g_r.at[5 + 2 * j], to_yp)
        b = ghalf(c, yp, zs[j], False)
        send(b, b, g_s.at[13 + 2 * j], g_r.at[13 + 2 * j], to_ym)

    gall[c, zh % 2, y * 2 + zh // 2] = g[...]
    own = gblk(c, y, zh)
    send(own, own, g_s.at[0], g_r.at[0], to_hp)
    send(own, own, g_s.at[1], g_r.at[1], to_hm)
    g_y1(0)

    def a2a_start(src, dst, n):
        @pl.loop(1, 16)
        def _(j):
            d = (t + j) % 16
            copy(src.at[d], dst.at[t], a_s.at[n, j], a_r.at[n, j], (dp, d)).start()

    def a2a_wait(src, dst, n):
        dst[t] = src[t]

        @pl.loop(1, 16)
        def _(j):
            d = (t + 16 - j) % 16
            copy(src.at[d], dst.at[d], a_s.at[n, j], a_r.at[n, j], (dp, d)).wait()

    a2a_start(hs, r1, 0)

    @pl.loop(0, 14)
    def _(i):
        scale = 7.0 * jnp.exp2(ex[pl.ds(i, 1), :].astype(F32))
        inv = 1.0 / scale
        for half in range(2):
            rows = pl.ds(pl.multiple_of(i * 128 + half * 64, 64), 64)
            s = jnp.tanh(w[rows, :].astype(F32) * inv)
            wq[c, rows, :] = (scale * s).astype(BF16)
            dsq[rows, :] = 1.0 - s * s

    send(wq.at[c], wq.at[c], c_s.at[0], c_r.at[0], to_co)

    arrived(gblk(c, y, hm), g_s.at[0], g_r.at[0], to_hm)
    b = ghalf(c, y, hm, True)
    send(b, b, g_s.at[2], g_r.at[2], to_hp)
    g_y1(1)
    arrived(gblk(c, y, hp), g_s.at[1], g_r.at[1], to_hp)
    b = ghalf(c, y, hp, False)
    send(b, b, g_s.at[3], g_r.at[3], to_hm)
    g_y1(2)
    g_y2(0)
    arrived(ghalf(c, y, ho, True), g_s.at[2], g_r.at[2], to_hm)
    arrived(ghalf(c, y, ho, False), g_s.at[3], g_r.at[3], to_hp)
    g_y1(3)
    g_y2(1)
    g_y2(2)

    a2a_wait(hs, r1, 0)
    walsh_16(r1, s2)
    a2a_start(s2, r2, 1)

    g_y2(3)
    for j in range(4):
        arrived(ghalf(c, yo, zs[j], True), g_s.at[12 + 2 * j], g_r.at[12 + 2 * j], to_ym)
        arrived(ghalf(c, yo, zs[j], False), g_s.at[13 + 2 * j], g_r.at[13 + 2 * j], to_yp)

    b = gall.at[c, co]
    send(b, b, c_s.at[1], c_r.at[1], to_co)
    arrived(wq.at[co], c_s.at[0], c_r.at[0], to_co)
    arrived(gall.at[co, c], c_s.at[1], c_r.at[1], to_co)

    def partial(slot, xq):
        a0 = gall[0, c, pl.ds(2 * xq, 2)].reshape(256, FEAT)
        a1 = gall[1, c, pl.ds(2 * xq, 2)].reshape(256, FEAT)
        for n in range(7):
            cols = slice(n * 256, (n + 1) * 256)
            p = nt(a0, wq[0, cols, :]) + nt(a1, wq[1, cols, :])
            pbuf[slot, :, :, cols] = p.astype(BF16).reshape(2, ROWS, 256)

    def add_into(slot, z, src):
        @pl.loop(0, 8)
        def _(i):
            rows = pl.ds(pl.multiple_of(i * 16, 16), 16)
            pbuf[slot, z, rows, :] = (
                pbuf[slot, z, rows, :].astype(F32) + src[rows, :].astype(F32)
            ).astype(BF16)

    partial(2, xo)
    send(pbuf.at[2, zl], rsa.at[0], p_s.at[0], p_r.at[0], to_xp)
    send(pbuf.at[2, zo], rsa.at[1], p_s.at[1], p_r.at[1], to_xm)
    partial(1, xp)
    send(pbuf.at[1, zo], rsb.at[0, 0], p_s.at[2], p_r.at[2], to_xp)
    partial(3, xm)
    send(pbuf.at[3, zl], rsb.at[1, 1], p_s.at[3], p_r.at[3], to_xm)
    partial(0, x)

    def local_walsh(src):
        for m in range(COS):
            j, k = m // 7, m % 7
            blk = jnp.concatenate([src[2 * i + j, :, 128 * k:128 * k + 128] for i in range(8)], axis=0)
            uu[m] = jnp.dot(blk, hw[...], preferred_element_type=F32)

    a2a_wait(s2, r2, 1)
    local_walsh(r2)
    me = 2 * x + zl

    @pl.loop(0, 8)
    def _(i):
        rows = pl.ds(pl.multiple_of(i * 16, 16), 16)
        u = [uu[m, rows, :] for m in range(COS)]
        ev = [u[m] + u[13 - m] for m in range(7)]
        od = [u[m] - u[13 - m] for m in range(7)]
        for n in range(COS):
            part = od if n % 2 else ev
            acc = part[0] * float(COSINE[0, n])
            for m in range(1, 7):
                acc = acc + part[m] * float(COSINE[m, n])
            rot[c, me, rows, 128 * n:128 * n + 128] = acc.astype(BF16)

    def rblk(xx, zz, cc):
        return rot.at[cc, 2 * xx + zz]

    def to_sibling(n, xx, zz):
        b = rblk(xx, zz, c)
        send(b, b, k_s.at[7 + n], k_r.at[7 + n], to_co)

    def gather(n, xx, zz, dev):
        b = rblk(xx, zz, c)
        send(b, b, k_s.at[n], k_r.at[n], dev)

    def gathered(n, xx, zz, dev):
        arrived(rblk(xx, zz, c), k_s.at[n], k_r.at[n], dev)

    gather(0, x, zl, to_zl)
    to_sibling(0, x, zl)

    arrived(rsa.at[0], p_s.at[0], p_r.at[0], to_xm)
    add_into(1, zl, rsa.at[0])
    send(pbuf.at[1, zl], rsb.at[0, 1], p_s.at[4], p_r.at[4], to_xp)
    arrived(rsa.at[1], p_s.at[1], p_r.at[1], to_xp)
    add_into(3, zo, rsa.at[1])
    send(pbuf.at[3, zo], rsb.at[1, 0], p_s.at[5], p_r.at[5], to_xm)

    gather(1, x, zl, to_xp)
    gather(4, x, zl, to_xm)
    gathered(0, x, zo, to_zl)
    gather(2, x, zo, to_xp)
    gather(5, x, zo, to_xm)
    to_sibling(1, x, zo)

    arrived(rsb.at[0, 0], p_s.at[2], p_r.at[2], to_xm)
    arrived(rsb.at[1, 0], p_s.at[5], p_r.at[5], to_xp)

    @pl.loop(0, 8)
    def _(i):
        rows = pl.ds(pl.multiple_of(i * 16, 16), 16)
        zsnd[rows, :] = (
            pbuf[0, zo, rows, :].astype(F32)
            + rsb[0, 0, rows, :].astype(F32)
            + rsb[1, 0, rows, :].astype(F32)
        ).astype(BF16)

    send(zsnd, zrcv, p_s.at[6], p_r.at[6], to_zl)

    arrived(rsb.at[0, 1], p_s.at[4], p_r.at[4], to_xm)
    arrived(rsb.at[1, 1], p_s.at[3], p_r.at[3], to_xp)
    arrived(zrcv, p_s.at[6], p_r.at[6], to_zl)

    @pl.loop(0, 8)
    def _(i):
        rows = pl.ds(pl.multiple_of(i * 16, 16), 16)
        s = (
            pbuf[0, zl, rows, :].astype(F32)
            + rsb[0, 1, rows, :].astype(F32)
            + rsb[1, 1, rows, :].astype(F32)
            + zrcv[rows, :].astype(F32)
        ).astype(BF16)
        hb[2 * i] = s[:, :HALF]
        hb[2 * i + 1] = s[:, HALF:]

    a2a_start(hb, r3, 2)

    gathered(1, xm, zl, to_xm)
    gather(3, xm, zl, to_xp)
    to_sibling(2, xm, zl)
    gathered(4, xp, zl, to_xp)
    to_sibling(3, xp, zl)
    gathered(5, xp, zo, to_xp)
    gather(6, xp, zo, to_xm)
    to_sibling(4, xp, zo)
    gathered(2, xm, zo, to_xm)
    to_sibling(5, xm, zo)

    a2a_wait(hb, r3, 2)
    walsh_16(r3, s4)
    a2a_start(s4, r4, 3)

    def project(yq):
        for par in range(2):
            a = rot[par, pl.ds(2 * yq, 2)].reshape(256, WIDTH)
            for n in range(2):
                cols = slice(n * 256, n * 256 + 256)
                p = jnp.dot(a, wq[c, :, cols], preferred_element_type=F32)
                lo[yq, par, :, :, cols] = p.astype(BF16).reshape(2, ROWS, 256)

    gathered(3, xo, zl, to_xm)
    to_sibling(6, xo, zl)
    gathered(6, xo, zo, to_xp)
    to_sibling(7, xo, zo)

    for n, (xx, zz) in enumerate(
        ((x, zl), (x, zo), (xm, zl), (xp, zl), (xp, zo), (xm, zo), (xo, zl), (xo, zo))
    ):
        arrived(rblk(xx, zz, co), k_s.at[7 + n], k_r.at[7 + n], to_co)

    project(yo)
    send(lo.at[yo, 0], ta.at[0], t_s.at[0], t_r.at[0], to_yp)
    send(lo.at[yo, 1], ta.at[1], t_s.at[1], t_r.at[1], to_ym)
    project(yp)
    send(lo.at[yp, 1], tb.at[0, 1], t_s.at[2], t_r.at[2], to_yp)
    project(ym)
    send(lo.at[ym, 0], tb.at[1, 0], t_s.at[3], t_r.at[3], to_ym)

    arrived(ta.at[0], t_s.at[0], t_r.at[0], to_ym)
    lo[yp, 0] = (lo[yp, 0].astype(F32) + ta[0].astype(F32)).astype(BF16)
    send(lo.at[yp, 0], tb.at[0, 0], t_s.at[4], t_r.at[4], to_yp)
    arrived(ta.at[1], t_s.at[1], t_r.at[1], to_yp)
    lo[ym, 1] = (lo[ym, 1].astype(F32) + ta[1].astype(F32)).astype(BF16)
    send(lo.at[ym, 1], tb.at[1, 1], t_s.at[5], t_r.at[5], to_ym)
    project(y)

    def down(lo_n, hi_n):
        @pl.loop(lo_n, hi_n)
        def _(n):
            cols = pl.ds(pl.multiple_of(n * 256, 256), 256)
            acc = None
            for par in range(2):
                for q in range(2):
                    a = rot[par, 4 * q:4 * q + 4, :, cols].reshape(512, 256)
                    p = tn(a, gall[c, par, 4 * q:4 * q + 4].reshape(512, FEAT))
                    acc = p if acc is None else acc + p
            gd_out[cols, :] = acc * dsq[cols, :]

    down(0, 4)

    for par in range(2):
        i = 2 + 2 * par
        arrived(tb.at[0, 1 - par], t_s.at[i], t_r.at[i], to_ym)
        arrived(tb.at[1, par], t_s.at[i + 1], t_r.at[i + 1], to_yp)
    for par in range(2):
        lz[par] = (
            lo[y, par].astype(F32) + tb[0, par].astype(F32) + tb[1, par].astype(F32)
        ).astype(BF16)

    def lzh(hh, top):
        return lz.at[hh % 2, hh // 2, pl.ds(0 if top else 64, 64)]

    send(lzh(ho, True), tc.at[0], t_s.at[6], t_r.at[6], to_hp)
    send(lzh(ho, False), tc.at[1], t_s.at[7], t_r.at[7], to_hm)
    down(4, 6)
    arrived(tc.at[0], t_s.at[6], t_r.at[6], to_hm)
    v = lzh(hp, True)
    v[...] = (v[...].astype(F32) + tc[0].astype(F32)).astype(BF16)
    b = lz.at[hp % 2, hp // 2]
    send(b, td.at[0], t_s.at[8], t_r.at[8], to_hp)
    arrived(tc.at[1], t_s.at[7], t_r.at[7], to_hp)
    v = lzh(hm, False)
    v[...] = (v[...].astype(F32) + tc[1].astype(F32)).astype(BF16)
    b = lz.at[hm % 2, hm // 2]
    send(b, td.at[1], t_s.at[9], t_r.at[9], to_hm)
    down(6, 7)

    a2a_wait(s4, r4, 3)
    local_walsh(r4)

    @pl.loop(0, 8)
    def _(i):
        rows = pl.ds(pl.multiple_of(i * 16, 16), 16)
        for m in range(7):
            evn = uu[0, rows, :] * float(COSINE[m, 0])
            odd = uu[1, rows, :] * float(COSINE[m, 1])
            for n in range(2, COS, 2):
                evn = evn + uu[n, rows, :] * float(COSINE[m, n])
                odd = odd + uu[n + 1, rows, :] * float(COSINE[m, n + 1])
            for mm, val in ((m, evn + odd), (13 - m, evn - odd)):
                cols = slice(128 * mm, 128 * mm + 128)
                gh = val * sign[:, cols]
                v = gate[rows, cols].astype(F32)
                sigma = jax.nn.sigmoid(v)
                gg_out[rows, cols] = (
                    gh * up[rows, cols].astype(F32) * sigma * (1.0 + v * (1.0 - sigma))
                ).astype(BF16)
                gu_out[rows, cols] = (gh * (v * sigma)).astype(BF16)

    arrived(td.at[0], t_s.at[8], t_r.at[8], to_hm)
    arrived(td.at[1], t_s.at[9], t_r.at[9], to_hp)
    lo_out[...] = (
        lz[zh % 2, zh // 2].astype(F32) + td[0].astype(F32) + td[1].astype(F32)
    ).astype(BF16)

    for d in sent:
        d.wait_send()


def on_device(gate_pre, up_pre, down_rotated, exponents, signs, out_grad):
    vmem = pl.BlockSpec(memory_space=pltpu.VMEM)
    blocks = pltpu.VMEM((16, 16, HALF), BF16)
    dma = pltpu.SemaphoreType.DMA
    return pl.pallas_call(
        kernel,
        out_shape=(
            jax.ShapeDtypeStruct((ROWS, FEAT), BF16),
            jax.ShapeDtypeStruct((WIDTH, FEAT), F32),
            jax.ShapeDtypeStruct((ROWS, WIDTH), BF16),
            jax.ShapeDtypeStruct((ROWS, WIDTH), BF16),
        ),
        in_specs=[vmem] * 7,
        out_specs=(vmem,) * 4,
        scratch_shapes=[blocks] * 8
        + [
            pltpu.VMEM((COS, ROWS, WALSH), F32),
            pltpu.VMEM((2, 2, 8, ROWS, FEAT), BF16),
            pltpu.VMEM((2, WIDTH, FEAT), BF16),
            pltpu.VMEM((WIDTH, FEAT), F32),
            pltpu.VMEM((2, 8, ROWS, WIDTH), BF16),
            pltpu.VMEM((4, 2, ROWS, WIDTH), BF16),
            pltpu.VMEM((2, ROWS, WIDTH), BF16),
            pltpu.VMEM((2, 2, ROWS, WIDTH), BF16),
            pltpu.VMEM((ROWS, WIDTH), BF16),
            pltpu.VMEM((ROWS, WIDTH), BF16),
            pltpu.VMEM((4, 2, 2, ROWS, FEAT), BF16),
            pltpu.VMEM((2, 2, ROWS, FEAT), BF16),
            pltpu.VMEM((2, 2, 2, ROWS, FEAT), BF16),
            pltpu.VMEM((2, 2, ROWS, FEAT), BF16),
            pltpu.VMEM((2, 64, FEAT), BF16),
            pltpu.VMEM((2, ROWS, FEAT), BF16),
            dma((4, 16)), dma((4, 16)),
            dma((20,)), dma((20,)),
            dma((2,)), dma((2,)),
            dma((7,)), dma((7,)),
            dma((15,)), dma((15,)),
            dma((10,)), dma((10,)),
        ],
        compiler_params=pltpu.CompilerParams(
            collective_id=0, has_side_effects=True, vmem_limit_bytes=60 * 1024 * 1024
        ),
        cost_estimate=pl.CostEstimate(
            flops=11_300_000_000, bytes_accessed=9_000_000, transcendentals=2_000_000
        ),
    )(
        gate_pre, up_pre, down_rotated, exponents, signs.reshape(1, WIDTH), out_grad,
        jnp.asarray(walsh_signs(WALSH)),
    )


def solution(mesh):
    return jax.shard_map(
        on_device,
        mesh=mesh,
        in_specs=(
            P("dp", "tensor"),
            P("dp", "tensor"),
            P("tensor", "dp"),
            P("tensor", "dp"),
            P("tensor"),
            P("tensor", "dp"),
        ),
        out_specs=(P("tensor", "dp"), P("tensor", "dp"), P("dp", "tensor"), P("dp", "tensor")),
        check_vma=False,
    )
```

```python
import jax
import jax.numpy as jnp
import ml_dtypes
import numpy as np
from jax import lax
from jax.experimental import pallas as pl
from jax.experimental.pallas import tpu as pltpu
from jax.sharding import PartitionSpec as P

ROWS = 128
WIDTH = 1792
FEAT = 512
WALSH = 128
COS = 14
HALF = 896
WAVES = 4
WR = ROWS // WAVES
F32 = jnp.float32
BF16 = jnp.bfloat16
MESH = pl.DeviceIdType.MESH

COSINE = np.sqrt(2.0 / COS) * np.cos(
    np.pi * (2 * np.arange(COS)[:, None] + 1) * np.arange(COS)[None, :] / (2.0 * COS)
)
COSINE[:, 0] = np.sqrt(1.0 / COS)
COSINE = COSINE / np.sqrt(WALSH)


def walsh_signs(order):
    a = np.arange(order)[:, None] & np.arange(order)[None, :]
    parity = np.zeros((order, order), np.int64)
    for bit in range(order.bit_length()):
        parity = parity + (a >> bit & 1)
    return (1.0 - 2.0 * (parity % 2)).astype(ml_dtypes.bfloat16)


def walsh(order, src, dst):
    scale = 1.0 / np.sqrt(order)
    height, width = src.shape[1:]

    @pl.loop(0, height // 16)
    def _(i):
        rows = pl.ds(pl.multiple_of(i * 16, 16), 16)

        @pl.loop(0, width // 128)
        def _(ch):
            cols = pl.ds(pl.multiple_of(ch * 128, 128), 128)
            v = [src[k, rows, cols].astype(F32) for k in range(order)]
            step = 1
            while step < order:
                w = list(v)
                for k in range(order):
                    if not k & step:
                        w[k] = v[k] + v[k + step]
                        w[k + step] = v[k] - v[k + step]
                v = w
                step *= 2
            for k in range(order):
                dst[k, rows, cols] = (v[k] * scale).astype(BF16)


def nt(a, b):
    return lax.dot_general(a, b, (((1,), (1,)), ((), ())), preferred_element_type=F32)


def tn(a, b):
    return lax.dot_general(a, b, (((0,), (0,)), ((), ())), preferred_element_type=F32)


def kernel(
    gate_h, up_h, w_h, ex_h, sg_h, g_h, hw_h,
    lo_out, gd_out, gg_out, gu_out,
    gate, up, w, ex, sg, hw,
    f0, f1, f2, f3, f4, f5, f6, hb, r3, s4, r4, uu,
    gall, wq, dsq, rot,
    pbuf, rsa, rsb, zsnd, zrcv,
    lo, ta, tb, lz, tc, td,
    lov, gdv, ggv, guv,
    i_s, o_s, f_s, f_r, a_s, a_r, g_s, g_r, c_s, c_r, p_s, p_r, k_s, k_r, t_s, t_r,
):
    dp = lax.axis_index("dp")
    t = lax.axis_index("tensor")
    x, zl, c = dp // 4, (dp // 2) % 2, dp % 2
    y, zh = t // 4, t % 4
    xp, xm, xo = (x + 1) % 4, (x + 3) % 4, (x + 2) % 4
    yp, ym, yo = (y + 1) % 4, (y + 3) % 4, (y + 2) % 4
    hp, hm, ho = (zh + 1) % 4, (zh + 3) % 4, (zh + 2) % 4
    zo, co = 1 - zl, 1 - c
    to_xp = (xp * 4 + zl * 2 + c, t)
    to_xm = (xm * 4 + zl * 2 + c, t)
    to_zl = (x * 4 + zo * 2 + c, t)
    to_co = (x * 4 + zl * 2 + co, t)
    to_yp, to_ym = (dp, yp * 4 + zh), (dp, ym * 4 + zh)
    to_hp, to_hm = (dp, y * 4 + hp), (dp, y * 4 + hm)

    def copy(src, dst, ss, rs, dev):
        return pltpu.make_async_remote_copy(
            src_ref=src, dst_ref=dst, send_sem=ss, recv_sem=rs, device_id=dev, device_id_type=MESH
        )

    sent = []

    def send(src, dst, ss, rs, dev):
        d = copy(src, dst, ss, rs, dev)
        d.start()
        sent.append(d)

    def arrived(dst, ss, rs, dev):
        copy(dst, dst, ss, rs, dev).wait_recv()

    g_in = pltpu.make_async_copy(g_h, gall.at[c, zh % 2, y * 2 + zh // 2], i_s.at[0])
    g_in.start()
    loads = [
        pltpu.make_async_copy(src, dst, i_s.at[1 + n])
        for n, (src, dst) in enumerate(((sg_h, sg), (gate_h, gate), (up_h, up), (ex_h, ex), (w_h, w), (hw_h, hw)))
    ]
    barrier = pltpu.get_barrier_semaphore()

    @pl.loop(1, 16)
    def _(j):
        pl.semaphore_signal(barrier, inc=1, device_id=(dp, (t + j) % 16), device_id_type=MESH)

    for dev in (to_xp, to_xm, to_zl, to_co):
        pl.semaphore_signal(barrier, inc=1, device_id=dev, device_id_type=MESH)
    for d in loads:
        d.start()
    g_in.wait()
    pl.semaphore_wait(barrier, 19)

    def gblk(core, yy, hh):
        return gall.at[core, hh % 2, yy * 2 + hh // 2]

    def ghalf(core, yy, hh, top):
        return gall.at[core, hh % 2, yy * 2 + hh // 2, pl.ds(0 if top else 64, 64)]

    zs = (zh, hm, hp, ho)

    def g_z(n, hh, top, dev):
        b = ghalf(c, y, hh, top)
        send(b, b, g_s.at[n], g_r.at[n], dev)

    def g_zd(n, hh, top, dev):
        arrived(ghalf(c, y, hh, top), g_s.at[n], g_r.at[n], dev)

    def g_y1(j, top):
        n = 6 + 6 * j + (0 if top else 2)
        b = ghalf(c, y, zs[j], top)
        send(b, b, g_s.at[n], g_r.at[n], to_yp)
        send(b, b, g_s.at[n + 1], g_r.at[n + 1], to_ym)

    def g_yd(j, n, yy, top, dev):
        n = 6 + 6 * j + n
        arrived(ghalf(c, yy, zs[j], top), g_s.at[n], g_r.at[n], dev)

    def g_y2(j):
        n = 6 + 6 * j
        g_yd(j, 0, ym, True, to_ym)
        b = ghalf(c, ym, zs[j], True)
        send(b, b, g_s.at[n + 4], g_r.at[n + 4], to_yp)
        g_yd(j, 3, yp, False, to_yp)
        b = ghalf(c, yp, zs[j], False)
        send(b, b, g_s.at[n + 5], g_r.at[n + 5], to_ym)

    def g_core(n, yy):
        b = gall.at[c, co, pl.ds(2 * yy, 2)]
        send(b, b, c_s.at[1 + n], c_r.at[1 + n], to_co)

    def g_cored(n, yy):
        arrived(gall.at[co, c, pl.ds(2 * yy, 2)], c_s.at[1 + n], c_r.at[1 + n], to_co)

    g_z(0, zh, True, to_hp)
    g_z(1, zh, False, to_hm)
    g_y1(0, True)
    g_y1(0, False)
    g_z(2, zh, False, to_hp)
    g_z(3, zh, True, to_hm)

    for d in loads[:3]:
        d.wait()
    sign = jnp.concatenate([sg[pl.ds(128 * m, 128)].reshape(1, 128) for m in range(COS)], axis=1)
    sign = 2.0 * sign.astype(F32) - 1.0

    @pl.loop(0, 8)
    def _(i):
        rows = pl.ds(pl.multiple_of(i * 16, 16), 16)
        v = gate[rows, :].astype(F32)
        h = (v * jax.nn.sigmoid(v) * up[rows, :].astype(F32)).astype(BF16).astype(F32)
        f0[i // 2, pl.ds(pl.multiple_of(i % 2 * 16, 16), 16), :] = (h * sign).astype(BF16)

    def stage_dev(n, d):
        return (dp, y * 4 + d) if n < 2 else (dp, d * 4 + zh)

    def stage_start(src, dst, n):
        me = zh if n < 2 else y
        for j in range(1, 4):
            d = (me + j) % 4
            copy(src.at[d], dst.at[me], f_s.at[n, j], f_r.at[n, j], stage_dev(n, d)).start()

    def stage_wait(src, dst, n):
        me = zh if n < 2 else y
        dst[me] = src[me]
        for j in range(1, 4):
            d = (me + 4 - j) % 4
            copy(src.at[d], dst.at[d], f_s.at[n, j], f_r.at[n, j], stage_dev(n, d)).wait()

    g_zd(0, hm, True, to_hm)
    g_z(4, hm, True, to_hp)
    g_y1(1, True)
    g_zd(1, hp, False, to_hp)
    g_z(5, hp, False, to_hm)
    g_y1(2, False)
    g_y2(0)
    g_zd(2, hm, False, to_hm)
    g_y1(1, False)
    g_zd(3, hp, True, to_hp)
    g_y1(2, True)
    stage_start(f0, f1, 0)

    for d in loads[3:]:
        d.wait()

    @pl.loop(0, 14)
    def _(i):
        scale = 7.0 * jnp.exp2(ex[pl.ds(i, 1), :].astype(F32))
        inv = 1.0 / scale
        for half in range(2):
            rows = pl.ds(pl.multiple_of(i * 128 + half * 64, 64), 64)
            s = jnp.tanh(w[rows, :].astype(F32) * inv)
            wq[c, rows, :] = (scale * s).astype(BF16)
            dsq[rows, :] = 1.0 - s * s

    send(wq.at[c], wq.at[c], c_s.at[0], c_r.at[0], to_co)

    g_zd(4, ho, True, to_hm)
    g_y1(3, True)
    g_zd(5, ho, False, to_hp)
    g_y1(3, False)
    g_core(0, y)
    g_y2(1)
    g_y2(2)

    def a2a_start(src, dst, n):
        @pl.loop(1, 16)
        def _(j):
            d = (t + j) % 16
            copy(src.at[d], dst.at[t], a_s.at[n, j], a_r.at[n, j], (dp, d)).start()

    def a2a_wait(src, dst, n):
        dst[t] = src[t]

        @pl.loop(1, 16)
        def _(j):
            d = (t + 16 - j) % 16
            copy(src.at[d], dst.at[d], a_s.at[n, j], a_r.at[n, j], (dp, d)).wait()

    top, low = pl.ds(0, 64), pl.ds(64, 64)

    def add_into(slot, z, half, src):
        @pl.loop(0, 4)
        def _(i):
            here = pl.ds(pl.multiple_of(i * 16, 16), 16)
            rows = pl.ds(pl.multiple_of(half * 64 + i * 16, 16), 16)
            pbuf[slot, z, rows, :] = (
                pbuf[slot, z, rows, :].astype(F32) + src[here, :].astype(F32)
            ).astype(BF16)

    def p_copy(k, n, src, dst, dev):
        return copy(src, dst, p_s.at[6 * k + n], p_r.at[6 * k + n], dev)

    p_far, p_next, p_last = [], [], []
    for k, z in ((0, zo), (1, zl)):
        p_far.append(p_copy(k, 0, pbuf.at[2, z, top], rsa.at[k, 0], to_xp))
        p_far.append(p_copy(k, 1, pbuf.at[2, z, low], rsa.at[k, 1], to_xm))
        p_next.append(p_copy(k, 2, pbuf.at[1, z, low], rsb.at[k, 0, low], to_xp))
        p_last.append(p_copy(k, 3, pbuf.at[3, z, top], rsb.at[k, 1, top], to_xm))
    sent.extend((*p_far, *p_next, *p_last))

    def p_onward(k, z):
        p_copy(k, 0, rsa.at[k, 0], rsa.at[k, 0], to_xm).wait_recv()
        add_into(1, z, 0, rsa.at[k, 0])
        d = p_copy(k, 4, pbuf.at[1, z, top], rsb.at[k, 0, top], to_xp)
        d.start()
        sent.append(d)
        p_copy(k, 1, rsa.at[k, 1], rsa.at[k, 1], to_xp).wait_recv()
        add_into(3, z, 1, rsa.at[k, 1])
        d = p_copy(k, 5, pbuf.at[3, z, low], rsb.at[k, 1, low], to_xm)
        d.start()
        sent.append(d)

    def p_arrived(k):
        p_copy(k, 2, rsb.at[k, 0, low], rsb.at[k, 0, low], to_xm).wait_recv()
        p_copy(k, 3, rsb.at[k, 1, top], rsb.at[k, 1, top], to_xp).wait_recv()
        p_copy(k, 4, rsb.at[k, 0, top], rsb.at[k, 0, top], to_xm).wait_recv()
        p_copy(k, 5, rsb.at[k, 1, low], rsb.at[k, 1, low], to_xp).wait_recv()

    def partial(n, q):
        g_cored(n, q)
        slot = (q + 4 - x) % 4
        a0 = gall[0, c, pl.ds(2 * q, 2)].reshape(256, FEAT)
        a1 = gall[1, c, pl.ds(2 * q, 2)].reshape(256, FEAT)
        for n in range(7):
            cols = slice(n * 256, (n + 1) * 256)
            p = nt(a0, wq[0, cols, :]) + nt(a1, wq[1, cols, :])
            pbuf[slot, :, :, cols] = p.astype(BF16).reshape(2, ROWS, 256)

        @pl.when(slot == 2)
        def _():
            p_far[0].start()
            p_far[1].start()

        @pl.when(slot == 1)
        def _():
            p_next[0].start()

        @pl.when(slot == 3)
        def _():
            p_last[0].start()

    arrived(wq.at[co], c_s.at[0], c_r.at[0], to_co)
    partial(0, y)
    g_y2(3)
    for j in range(4):
        g_yd(j, 2, ym, False, to_ym)
        g_yd(j, 1, yp, True, to_yp)
    g_core(1, ym)
    g_core(2, yp)
    partial(1, ym)
    partial(2, yp)
    for j in range(4):
        g_yd(j, 4, yo, True, to_ym)
        g_yd(j, 5, yo, False, to_yp)
    g_core(3, yo)
    partial(3, yo)
    stage_wait(f0, f1, 0)
    walsh(4, f1, f2)
    stage_start(f2, f3, 1)
    p_onward(0, zo)
    for d in (p_far[2], p_far[3], p_next[1], p_last[1]):
        d.start()
    stage_wait(f2, f3, 1)
    stage_start(f3, f4, 2)

    p_arrived(0)

    @pl.loop(0, 8)
    def _(i):
        rows = pl.ds(pl.multiple_of(i * 16, 16), 16)
        zsnd[rows, :] = (
            pbuf[0, zo, rows, :].astype(F32)
            + rsb[0, 0, rows, :].astype(F32)
            + rsb[0, 1, rows, :].astype(F32)
        ).astype(BF16)

    send(zsnd, zrcv, p_s.at[12], p_r.at[12], to_zl)
    stage_wait(f3, f4, 2)
    walsh(4, f4, f5)
    stage_start(f5, f6, 3)
    p_onward(1, zl)
    stage_wait(f5, f6, 3)

    def local_walsh(block):
        for m in range(COS):
            uu[m] = jnp.dot(block(m), hw[...], preferred_element_type=F32)

    local_walsh(lambda m: f6[:, :, 128 * m:128 * m + 128].reshape(ROWS, WALSH))
    me = 2 * x + zl

    @pl.loop(0, 8)
    def _(i):
        rows = pl.ds(pl.multiple_of(i * 16, 16), 16)
        u = [uu[m, rows, :] for m in range(COS)]
        ev = [u[m] + u[13 - m] for m in range(7)]
        od = [u[m] - u[13 - m] for m in range(7)]
        for n in range(COS):
            part = od if n % 2 else ev
            acc = part[0] * float(COSINE[0, n])
            for m in range(1, 7):
                acc = acc + part[m] * float(COSINE[m, n])
            rot[c, me, rows, 128 * n:128 * n + 128] = acc.astype(BF16)

    def rblk(h, xx, zz, cc):
        return rot.at[cc, 2 * xx + zz, pl.ds(WR * h, WR)]

    def to_sibling(h, n, xx, zz):
        b = rblk(h, xx, zz, c)
        send(b, b, k_s.at[15 * h + 7 + n], k_r.at[15 * h + 7 + n], to_co)

    def gather(h, n, xx, zz, dev):
        b = rblk(h, xx, zz, c)
        send(b, b, k_s.at[15 * h + n], k_r.at[15 * h + n], dev)

    def gathered(h, n, xx, zz, dev):
        arrived(rblk(h, xx, zz, c), k_s.at[15 * h + n], k_r.at[15 * h + n], dev)

    def gather_zl(h):
        gather(h, 0, x, zl, to_zl)
        to_sibling(h, 0, x, zl)

    def gather_own(h):
        gather(h, 1, x, zl, to_xp)
        gather(h, 4, x, zl, to_xm)

    def gather_partner(h):
        gathered(h, 0, x, zo, to_zl)
        gather(h, 2, x, zo, to_xp)
        gather(h, 5, x, zo, to_xm)
        to_sibling(h, 1, x, zo)

    def gather_on(h):
        gathered(h, 1, xm, zl, to_xm)
        gather(h, 3, xm, zl, to_xp)
        to_sibling(h, 2, xm, zl)
        gathered(h, 4, xp, zl, to_xp)
        to_sibling(h, 3, xp, zl)
        gathered(h, 5, xp, zo, to_xp)
        gather(h, 6, xp, zo, to_xm)
        to_sibling(h, 4, xp, zo)
        gathered(h, 2, xm, zo, to_xm)
        to_sibling(h, 5, xm, zo)

    def gather_end(h):
        gathered(h, 3, xo, zl, to_xm)
        to_sibling(h, 6, xo, zl)
        gathered(h, 6, xo, zo, to_xp)
        to_sibling(h, 7, xo, zo)
        for n, (xx, zz) in enumerate(
            ((x, zl), (x, zo), (xm, zl), (xp, zl), (xp, zo), (xm, zo), (xo, zl), (xo, zo))
        ):
            arrived(rblk(h, xx, zz, co), k_s.at[15 * h + 7 + n], k_r.at[15 * h + 7 + n], to_co)

    for h in range(WAVES):
        gather_zl(h)
    gather_own(0)
    gather_own(1)

    def rotate_back():
        p_arrived(1)
        arrived(zrcv, p_s.at[12], p_r.at[12], to_zl)

        @pl.loop(0, 8)
        def _(i):
            rows = pl.ds(pl.multiple_of(i * 16, 16), 16)
            s = (
                pbuf[0, zl, rows, :].astype(F32)
                + rsb[1, 0, rows, :].astype(F32)
                + rsb[1, 1, rows, :].astype(F32)
                + zrcv[rows, :].astype(F32)
            ).astype(BF16)
            hb[2 * i] = s[:, :HALF]
            hb[2 * i + 1] = s[:, HALF:]

        a2a_start(hb, r3, 0)

    def project(h):
        @pl.loop(0, 2)
        def _(par):
            a = rot[par, :, WR * h:WR * h + WR].reshape(8 * WR, WIDTH)
            for n in range(2):
                cols = slice(n * 256, n * 256 + 256)
                p = jnp.dot(a, wq[c, :, cols], preferred_element_type=F32)
                lo[h, par, :, :, cols] = p.astype(BF16).reshape(8, WR, 256)

    def lob(h, yy, par):
        return lo.at[h, par, pl.ds(2 * yy, 2)]

    def tsend(h, n, src, dst, dev):
        send(src, dst, t_s.at[10 * h + n], t_r.at[10 * h + n], dev)

    def tarrived(h, n, dst, dev):
        arrived(dst, t_s.at[10 * h + n], t_r.at[10 * h + n], dev)

    def out_y1(h):
        project(h)
        tsend(h, 0, lob(h, yo, 0), ta.at[h, 0], to_yp)
        tsend(h, 1, lob(h, yo, 1), ta.at[h, 1], to_ym)
        tsend(h, 2, lob(h, yp, 1), tb.at[h, 0, 1], to_yp)
        tsend(h, 3, lob(h, ym, 0), tb.at[h, 1, 0], to_ym)

    def add_to(v, u):
        v[...] = (v[...].astype(F32) + u[...].astype(F32)).astype(BF16)

    def out_y2(h):
        tarrived(h, 0, ta.at[h, 0], to_ym)
        add_to(lob(h, yp, 0), ta.at[h, 0])
        tsend(h, 4, lob(h, yp, 0), tb.at[h, 0, 0], to_yp)
        tarrived(h, 1, ta.at[h, 1], to_yp)
        add_to(lob(h, ym, 1), ta.at[h, 1])
        tsend(h, 5, lob(h, ym, 1), tb.at[h, 1, 1], to_ym)

    def lzh(h, hh, left):
        return lz.at[h, hh % 2, hh // 2, :, pl.ds(0 if left else 256, 256)]

    def out_z1(h):
        tarrived(h, 2, tb.at[h, 0, 1], to_ym)
        tarrived(h, 3, tb.at[h, 1, 0], to_yp)
        tarrived(h, 4, tb.at[h, 0, 0], to_ym)
        tarrived(h, 5, tb.at[h, 1, 1], to_yp)
        for par in range(2):
            lz[h, par] = (
                lob(h, y, par)[...].astype(F32) + tb[h, 0, par].astype(F32) + tb[h, 1, par].astype(F32)
            ).astype(BF16)
        tsend(h, 6, lzh(h, ho, True), tc.at[h, 0], to_hp)
        tsend(h, 7, lzh(h, ho, False), tc.at[h, 1], to_hm)

    def out_z2(h):
        tarrived(h, 6, tc.at[h, 0], to_hm)
        add_to(lzh(h, hp, True), tc.at[h, 0])
        tsend(h, 8, lz.at[h, hp % 2, hp // 2], td.at[h, 0], to_hp)
        tarrived(h, 7, tc.at[h, 1], to_hp)
        add_to(lzh(h, hm, False), tc.at[h, 1])
        tsend(h, 9, lz.at[h, hm % 2, hm // 2], td.at[h, 1], to_hm)

    def out_end(h):
        tarrived(h, 8, td.at[h, 0], to_hm)
        tarrived(h, 9, td.at[h, 1], to_hp)
        lov[WR * h:WR * h + WR, :] = (
            lz[h, zh % 2, zh // 2].astype(F32) + td[h, 0].astype(F32) + td[h, 1].astype(F32)
        ).astype(BF16)

    def down(half, lo_n, hi_n):
        @pl.loop(lo_n, hi_n)
        def _(n):
            cols = pl.ds(pl.multiple_of(n * 256, 256), 256)
            acc = None
            for par in range(2):
                a = rot[par, :, 64 * half:64 * half + 64, cols].reshape(512, 256)
                p = tn(a, gall[c, par, :, 64 * half:64 * half + 64].reshape(512, FEAT))
                acc = p if acc is None else acc + p
            gdv[cols, :] = acc if half == 0 else (gdv[cols, :] + acc) * dsq[cols, :]

    stores = []

    def store(src, dst):
        d = pltpu.make_async_copy(src, dst, o_s.at[len(stores)])
        d.start()
        stores.append(d)

    rotate_back()
    gather_partner(0)
    gather_on(0)
    gather_own(2)
    gather_partner(1)
    gather_end(0)
    out_y1(0)
    gather_on(1)
    gather_own(3)
    gather_partner(2)
    gather_end(1)
    out_y1(1)
    out_y2(0)
    a2a_wait(hb, r3, 0)
    walsh(16, r3, s4)
    a2a_start(s4, r4, 1)
    gather_on(2)
    gather_partner(3)
    gather_end(2)
    out_y1(2)
    out_z1(0)
    out_y2(1)
    gather_on(3)
    down(0, 0, 7)
    out_z2(0)
    out_z1(1)
    out_y2(2)
    gather_end(3)
    out_y1(3)
    out_z2(1)
    out_z1(2)
    down(1, 0, 3)
    out_y2(3)
    out_z2(2)
    down(1, 3, 4)
    store(gdv.at[pl.ds(0, 1024)], gd_out.at[pl.ds(0, 1024)])
    out_z1(3)
    down(1, 4, 7)
    store(gdv.at[pl.ds(1024, 768)], gd_out.at[pl.ds(1024, 768)])
    out_z2(3)
    a2a_wait(s4, r4, 1)

    def block_of(m):
        j, k = m // 7, m % 7
        return jnp.concatenate([r4[2 * i + j, :, 128 * k:128 * k + 128] for i in range(8)], axis=0)

    local_walsh(block_of)

    @pl.loop(0, 8)
    def _(i):
        rows = pl.ds(pl.multiple_of(i * 16, 16), 16)
        for m in range(7):
            evn = uu[0, rows, :] * float(COSINE[m, 0])
            odd = uu[1, rows, :] * float(COSINE[m, 1])
            for n in range(2, COS, 2):
                evn = evn + uu[n, rows, :] * float(COSINE[m, n])
                odd = odd + uu[n + 1, rows, :] * float(COSINE[m, n + 1])
            for mm, val in ((m, evn + odd), (13 - m, evn - odd)):
                cols = slice(128 * mm, 128 * mm + 128)
                gh = val * sign[:, cols]
                v = gate[rows, cols].astype(F32)
                sigma = jax.nn.sigmoid(v)
                ggv[rows, cols] = (
                    gh * up[rows, cols].astype(F32) * sigma * (1.0 + v * (1.0 - sigma))
                ).astype(BF16)
                guv[rows, cols] = (gh * (v * sigma)).astype(BF16)

    store(ggv, gg_out)
    store(guv, gu_out)
    for h in range(WAVES):
        out_end(h)
    store(lov, lo_out)
    for d in sent:
        d.wait_send()
    for d in stores:
        d.wait()


def finish(lo_i, gd_i, gg_i, gu_i, lo_o, gd_o, gg_o, gu_o, lo_v, gd_v, gg_v, gu_v, sem_i, sem_o):
    pieces = []
    for n in range(7):
        rows = pl.ds(256 * n, 256)
        pieces.append((gd_i.at[rows], gd_v.at[rows], gd_o.at[rows]))
    pieces += [(gg_i, gg_v, gg_o), (gu_i, gu_v, gu_o), (lo_i, lo_v, lo_o)]
    loads = [pltpu.make_async_copy(a, b, sem_i.at[n]) for n, (a, b, _) in enumerate(pieces)]
    stores = [pltpu.make_async_copy(b, o, sem_o.at[n]) for n, (_, b, o) in enumerate(pieces)]
    for d in loads:
        d.start()
    for d, e in zip(loads, stores):
        d.wait()
        e.start()
    for e in stores:
        e.wait()


def on_device(gate_pre, up_pre, down_rotated, exponents, signs, out_grad):
    anywhere = pl.BlockSpec(memory_space=pl.ANY)
    blocks = pltpu.VMEM((16, 16, HALF), BF16)
    dma = pltpu.SemaphoreType.DMA
    out_shape = (
        jax.ShapeDtypeStruct((ROWS, FEAT), BF16),
        jax.ShapeDtypeStruct((WIDTH, FEAT), F32),
        jax.ShapeDtypeStruct((ROWS, WIDTH), BF16),
        jax.ShapeDtypeStruct((ROWS, WIDTH), BF16),
    )
    outs = pl.pallas_call(
        kernel,
        out_shape=out_shape,
        in_specs=[anywhere] * 7,
        out_specs=(anywhere,) * 4,
        scratch_shapes=[
            pltpu.VMEM((ROWS, WIDTH), BF16),
            pltpu.VMEM((ROWS, WIDTH), BF16),
            pltpu.VMEM((WIDTH, FEAT), BF16),
            pltpu.VMEM((COS, FEAT), jnp.int32),
            pltpu.VMEM((WIDTH,), jnp.int32),
            pltpu.VMEM((WALSH, WALSH), BF16),
        ]
        + [pltpu.VMEM((4, 32, WIDTH), BF16)] * 7
        + [blocks] * 4
        + [
            pltpu.VMEM((COS, ROWS, WALSH), F32),
            pltpu.VMEM((2, 2, 8, ROWS, FEAT), BF16),
            pltpu.VMEM((2, WIDTH, FEAT), BF16),
            pltpu.VMEM((WIDTH, FEAT), F32),
            pltpu.VMEM((2, 8, ROWS, WIDTH), BF16),
            pltpu.VMEM((4, 2, ROWS, WIDTH), BF16),
            pltpu.VMEM((2, 2, 64, WIDTH), BF16),
            pltpu.VMEM((2, 2, ROWS, WIDTH), BF16),
            pltpu.VMEM((ROWS, WIDTH), BF16),
            pltpu.VMEM((ROWS, WIDTH), BF16),
            pltpu.VMEM((WAVES, 2, 8, WR, FEAT), BF16),
            pltpu.VMEM((WAVES, 2, 2, WR, FEAT), BF16),
            pltpu.VMEM((WAVES, 2, 2, 2, WR, FEAT), BF16),
            pltpu.VMEM((WAVES, 2, 2, WR, FEAT), BF16),
            pltpu.VMEM((WAVES, 2, WR, 256), BF16),
            pltpu.VMEM((WAVES, 2, WR, FEAT), BF16),
            pltpu.VMEM((ROWS, FEAT), BF16),
            pltpu.VMEM((WIDTH, FEAT), F32),
            pltpu.VMEM((ROWS, WIDTH), BF16),
            pltpu.VMEM((ROWS, WIDTH), BF16),
            dma((7,)), dma((5,)),
            dma((4, 4)), dma((4, 4)),
            dma((2, 16)), dma((2, 16)),
            dma((30,)), dma((30,)),
            dma((5,)), dma((5,)),
            dma((13,)), dma((13,)),
            dma((15 * WAVES,)), dma((15 * WAVES,)),
            dma((10 * WAVES,)), dma((10 * WAVES,)),
        ],
        compiler_params=pltpu.CompilerParams(
            collective_id=0, has_side_effects=True, vmem_limit_bytes=60 * 1024 * 1024
        ),
        cost_estimate=pl.CostEstimate(
            flops=11_300_000_000, bytes_accessed=9_000_000, transcendentals=2_000_000
        ),
    )(
        gate_pre, up_pre, down_rotated, exponents, signs, out_grad,
        jnp.asarray(walsh_signs(WALSH)),
    )
    return pl.pallas_call(
        finish,
        out_shape=out_shape,
        in_specs=[anywhere] * 4,
        out_specs=(anywhere,) * 4,
        scratch_shapes=[pltpu.VMEM(o.shape, o.dtype) for o in out_shape] + [dma((10,)), dma((10,))],
        compiler_params=pltpu.CompilerParams(vmem_limit_bytes=60 * 1024 * 1024),
    )(*outs)


def solution(mesh):
    return jax.shard_map(
        on_device,
        mesh=mesh,
        in_specs=(
            P("dp", "tensor"),
            P("dp", "tensor"),
            P("tensor", "dp"),
            P("tensor", "dp"),
            P("tensor"),
            P("tensor", "dp"),
        ),
        out_specs=(P("tensor", "dp"), P("tensor", "dp"), P("dp", "tensor"), P("dp", "tensor")),
        check_vma=False,
    )
```

```python
import jax
import jax.numpy as jnp
import ml_dtypes
import numpy as np
from jax import lax
from jax.experimental import pallas as pl
from jax.experimental.pallas import tpu as pltpu
from jax.sharding import PartitionSpec as P

ROWS = 128
WIDTH = 1792
FEAT = 512
WALSH = 128
COS = 14
HALF = 896
WAVES = 4
WR = ROWS // WAVES
F32 = jnp.float32
BF16 = jnp.bfloat16
MESH = pl.DeviceIdType.MESH

COSINE = np.sqrt(2.0 / COS) * np.cos(
    np.pi * (2 * np.arange(COS)[:, None] + 1) * np.arange(COS)[None, :] / (2.0 * COS)
)
COSINE[:, 0] = np.sqrt(1.0 / COS)
COSINE = COSINE / np.sqrt(WALSH)


def walsh_signs(order):
    a = np.arange(order)[:, None] & np.arange(order)[None, :]
    parity = np.zeros((order, order), np.int64)
    for bit in range(order.bit_length()):
        parity = parity + (a >> bit & 1)
    return (1.0 - 2.0 * (parity % 2)).astype(ml_dtypes.bfloat16)


def walsh(order, src, dst):
    scale = 1.0 / np.sqrt(order)
    height, width = src.shape[1:]

    @pl.loop(0, height // 16)
    def _(i):
        rows = pl.ds(pl.multiple_of(i * 16, 16), 16)

        @pl.loop(0, width // 128)
        def _(ch):
            cols = pl.ds(pl.multiple_of(ch * 128, 128), 128)
            v = [src[k, rows, cols].astype(F32) for k in range(order)]
            step = 1
            while step < order:
                w = list(v)
                for k in range(order):
                    if not k & step:
                        w[k] = v[k] + v[k + step]
                        w[k + step] = v[k] - v[k + step]
                v = w
                step *= 2
            for k in range(order):
                dst[k, rows, cols] = (v[k] * scale).astype(BF16)


def nt(a, b):
    return lax.dot_general(a, b, (((1,), (1,)), ((), ())), preferred_element_type=F32)


def tn(a, b):
    return lax.dot_general(a, b, (((0,), (0,)), ((), ())), preferred_element_type=F32)


def kernel(
    gate_h, up_h, w_h, ex_h, sg_h, g_h, hw_h,
    lo_out, gd_out, gg_out, gu_out,
    gate, up, w, ex, sg, hw,
    f0, f1, f2, f3, f4, f5, f6, hb, r3, s4, r4, uu,
    gall, wq, dsq, rot,
    pbuf, rsa, rsb, zsnd, zrcv,
    lo, tb, lz, td,
    lov, gdv, ggv, guv,
    i_s, o_s, f_s, f_r, a_s, a_r, g_s, g_r, c_s, c_r, p_s, p_r, k_s, k_r, t_s, t_r,
):
    dp = lax.axis_index("dp")
    t = lax.axis_index("tensor")
    x, zl, c = dp // 4, (dp // 2) % 2, dp % 2
    y, zh = t // 4, t % 4
    xp, xm, xo = (x + 1) % 4, (x + 3) % 4, (x + 2) % 4
    yp, ym, yo = (y + 1) % 4, (y + 3) % 4, (y + 2) % 4
    hp, hm, ho = (zh + 1) % 4, (zh + 3) % 4, (zh + 2) % 4
    zo, co = 1 - zl, 1 - c
    to_xp = (xp * 4 + zl * 2 + c, t)
    to_xm = (xm * 4 + zl * 2 + c, t)
    to_zl = (x * 4 + zo * 2 + c, t)
    to_co = (x * 4 + zl * 2 + co, t)
    to_yp, to_ym = (dp, yp * 4 + zh), (dp, ym * 4 + zh)
    to_hp, to_hm = (dp, y * 4 + hp), (dp, y * 4 + hm)

    def copy(src, dst, ss, rs, dev):
        return pltpu.make_async_remote_copy(
            src_ref=src, dst_ref=dst, send_sem=ss, recv_sem=rs, device_id=dev, device_id_type=MESH
        )

    sent = []

    def send(src, dst, ss, rs, dev):
        d = copy(src, dst, ss, rs, dev)
        d.start()
        sent.append(d)

    def arrived(dst, ss, rs, dev):
        copy(dst, dst, ss, rs, dev).wait_recv()

    g_in = pltpu.make_async_copy(g_h, gall.at[c, zh % 2, y * 2 + zh // 2], i_s.at[0])
    g_in.start()
    loads = [
        pltpu.make_async_copy(src, dst, i_s.at[1 + n])
        for n, (src, dst) in enumerate(((sg_h, sg), (gate_h, gate), (up_h, up), (ex_h, ex), (w_h, w), (hw_h, hw)))
    ]
    barrier = pltpu.get_barrier_semaphore()

    @pl.loop(1, 16)
    def _(j):
        pl.semaphore_signal(barrier, inc=1, device_id=(dp, (t + j) % 16), device_id_type=MESH)

    for dev in (to_xp, to_xm, to_zl, to_co):
        pl.semaphore_signal(barrier, inc=1, device_id=dev, device_id_type=MESH)
    for d in loads:
        d.start()
    g_in.wait()
    pl.semaphore_wait(barrier, 19)

    def gblk(core, yy, hh):
        return gall.at[core, hh % 2, yy * 2 + hh // 2]

    def ghalf(core, yy, hh, top):
        return gall.at[core, hh % 2, yy * 2 + hh // 2, pl.ds(0 if top else 64, 64)]

    zs = (zh, hm, hp, ho)

    def g_z(n, hh, top, dev):
        b = ghalf(c, y, hh, top)
        send(b, b, g_s.at[n], g_r.at[n], dev)

    def g_zd(n, hh, top, dev):
        arrived(ghalf(c, y, hh, top), g_s.at[n], g_r.at[n], dev)

    def g_y1(j, top):
        n = 6 + 6 * j + (0 if top else 2)
        b = ghalf(c, y, zs[j], top)
        send(b, b, g_s.at[n], g_r.at[n], to_yp)
        send(b, b, g_s.at[n + 1], g_r.at[n + 1], to_ym)

    def g_yd(j, n, yy, top, dev):
        n = 6 + 6 * j + n
        arrived(ghalf(c, yy, zs[j], top), g_s.at[n], g_r.at[n], dev)

    def g_y2(j):
        n = 6 + 6 * j
        g_yd(j, 0, ym, True, to_ym)
        b = ghalf(c, ym, zs[j], True)
        send(b, b, g_s.at[n + 4], g_r.at[n + 4], to_yp)
        g_yd(j, 3, yp, False, to_yp)
        b = ghalf(c, yp, zs[j], False)
        send(b, b, g_s.at[n + 5], g_r.at[n + 5], to_ym)

    def g_core(n, yy):
        b = gall.at[c, co, pl.ds(2 * yy, 2)]
        send(b, b, c_s.at[1 + n], c_r.at[1 + n], to_co)

    def g_cored(n, yy):
        arrived(gall.at[co, c, pl.ds(2 * yy, 2)], c_s.at[1 + n], c_r.at[1 + n], to_co)

    g_z(0, zh, True, to_hp)
    g_z(1, zh, False, to_hm)
    g_y1(0, True)
    g_y1(0, False)
    g_z(2, zh, False, to_hp)
    g_z(3, zh, True, to_hm)

    for d in loads[:3]:
        d.wait()
    sign = jnp.concatenate([sg[pl.ds(128 * m, 128)].reshape(1, 128) for m in range(COS)], axis=1)
    sign = 2.0 * sign.astype(F32) - 1.0

    @pl.loop(0, 8)
    def _(i):
        rows = pl.ds(pl.multiple_of(i * 16, 16), 16)
        v = gate[rows, :].astype(F32)
        h = (v * jax.nn.sigmoid(v) * up[rows, :].astype(F32)).astype(BF16).astype(F32)
        f0[i // 2, pl.ds(pl.multiple_of(i % 2 * 16, 16), 16), :] = (h * sign).astype(BF16)

    def stage_dev(n, d):
        return (dp, y * 4 + d) if n < 2 else (dp, d * 4 + zh)

    def stage_start(src, dst, n):
        me = zh if n < 2 else y
        for j in range(1, 4):
            d = (me + j) % 4
            copy(src.at[d], dst.at[me], f_s.at[n, j], f_r.at[n, j], stage_dev(n, d)).start()

    def stage_wait(src, dst, n):
        me = zh if n < 2 else y
        dst[me] = src[me]
        for j in range(1, 4):
            d = (me + 4 - j) % 4
            copy(src.at[d], dst.at[d], f_s.at[n, j], f_r.at[n, j], stage_dev(n, d)).wait()

    g_zd(0, hm, True, to_hm)
    g_z(4, hm, True, to_hp)
    g_y1(1, True)
    g_zd(1, hp, False, to_hp)
    g_z(5, hp, False, to_hm)
    g_y1(2, False)
    g_y2(0)
    g_zd(2, hm, False, to_hm)
    g_y1(1, False)
    g_zd(3, hp, True, to_hp)
    g_y1(2, True)
    stage_start(f0, f1, 0)

    for d in loads[3:]:
        d.wait()

    @pl.loop(0, 14)
    def _(i):
        scale = 7.0 * jnp.exp2(ex[pl.ds(i, 1), :].astype(F32))
        inv = 1.0 / scale
        for half in range(2):
            rows = pl.ds(pl.multiple_of(i * 128 + half * 64, 64), 64)
            s = jnp.tanh(w[rows, :].astype(F32) * inv)
            wq[c, rows, :] = (scale * s).astype(BF16)
            dsq[rows, :] = 1.0 - s * s

    send(wq.at[c], wq.at[c], c_s.at[0], c_r.at[0], to_co)

    g_zd(4, ho, True, to_hm)
    g_y1(3, True)
    g_zd(5, ho, False, to_hp)
    g_y1(3, False)
    g_core(0, y)
    g_y2(1)
    g_y2(2)

    def a2a_start(src, dst, n):
        @pl.loop(1, 16)
        def _(j):
            d = (t + j) % 16
            copy(src.at[d], dst.at[t], a_s.at[n, j], a_r.at[n, j], (dp, d)).start()

    def a2a_wait(src, dst, n):
        dst[t] = src[t]

        @pl.loop(1, 16)
        def _(j):
            d = (t + 16 - j) % 16
            copy(src.at[d], dst.at[d], a_s.at[n, j], a_r.at[n, j], (dp, d)).wait()

    top, low = pl.ds(0, 64), pl.ds(64, 64)

    def add_into(slot, z, half, src):
        @pl.loop(0, 4)
        def _(i):
            here = pl.ds(pl.multiple_of(i * 16, 16), 16)
            rows = pl.ds(pl.multiple_of(half * 64 + i * 16, 16), 16)
            pbuf[slot, z, rows, :] = (
                pbuf[slot, z, rows, :].astype(F32) + src[here, :].astype(F32)
            ).astype(BF16)

    def p_copy(k, n, src, dst, dev):
        return copy(src, dst, p_s.at[6 * k + n], p_r.at[6 * k + n], dev)

    p_far, p_next, p_last = [], [], []
    for k, z in ((0, zo), (1, zl)):
        p_far.append(p_copy(k, 0, pbuf.at[2, z, top], rsa.at[k, 0], to_xp))
        p_far.append(p_copy(k, 1, pbuf.at[2, z, low], rsa.at[k, 1], to_xm))
        p_next.append(p_copy(k, 2, pbuf.at[1, z, low], rsb.at[k, 0, low], to_xp))
        p_last.append(p_copy(k, 3, pbuf.at[3, z, top], rsb.at[k, 1, top], to_xm))
    sent.extend((*p_far, *p_next, *p_last))

    def p_onward(k, z):
        p_copy(k, 0, rsa.at[k, 0], rsa.at[k, 0], to_xm).wait_recv()
        add_into(1, z, 0, rsa.at[k, 0])
        d = p_copy(k, 4, pbuf.at[1, z, top], rsb.at[k, 0, top], to_xp)
        d.start()
        sent.append(d)
        p_copy(k, 1, rsa.at[k, 1], rsa.at[k, 1], to_xp).wait_recv()
        add_into(3, z, 1, rsa.at[k, 1])
        d = p_copy(k, 5, pbuf.at[3, z, low], rsb.at[k, 1, low], to_xm)
        d.start()
        sent.append(d)

    def p_arrived(k):
        p_copy(k, 2, rsb.at[k, 0, low], rsb.at[k, 0, low], to_xm).wait_recv()
        p_copy(k, 3, rsb.at[k, 1, top], rsb.at[k, 1, top], to_xp).wait_recv()
        p_copy(k, 4, rsb.at[k, 0, top], rsb.at[k, 0, top], to_xm).wait_recv()
        p_copy(k, 5, rsb.at[k, 1, low], rsb.at[k, 1, low], to_xp).wait_recv()

    def partial(n, q):
        g_cored(n, q)
        slot = (q + 4 - x) % 4
        a0 = gall[0, c, pl.ds(2 * q, 2)].reshape(256, FEAT)
        a1 = gall[1, c, pl.ds(2 * q, 2)].reshape(256, FEAT)
        for n in range(7):
            cols = slice(n * 256, (n + 1) * 256)
            p = nt(a0, wq[0, cols, :]) + nt(a1, wq[1, cols, :])
            pbuf[slot, :, :, cols] = p.astype(BF16).reshape(2, ROWS, 256)

        @pl.when(slot == 2)
        def _():
            p_far[0].start()
            p_far[1].start()

        @pl.when(slot == 1)
        def _():
            p_next[0].start()

        @pl.when(slot == 3)
        def _():
            p_last[0].start()

    arrived(wq.at[co], c_s.at[0], c_r.at[0], to_co)
    partial(0, y)
    g_y2(3)
    for j in range(4):
        g_yd(j, 2, ym, False, to_ym)
        g_yd(j, 1, yp, True, to_yp)
    g_core(1, ym)
    g_core(2, yp)
    partial(1, ym)
    partial(2, yp)
    for j in range(4):
        g_yd(j, 4, yo, True, to_ym)
        g_yd(j, 5, yo, False, to_yp)
    g_core(3, yo)
    partial(3, yo)
    stage_wait(f0, f1, 0)
    walsh(4, f1, f2)
    stage_start(f2, f3, 1)
    p_onward(0, zo)
    for d in (p_far[2], p_far[3], p_next[1], p_last[1]):
        d.start()
    stage_wait(f2, f3, 1)
    stage_start(f3, f4, 2)

    p_arrived(0)

    @pl.loop(0, 8)
    def _(i):
        rows = pl.ds(pl.multiple_of(i * 16, 16), 16)
        zsnd[rows, :] = (
            pbuf[0, zo, rows, :].astype(F32)
            + rsb[0, 0, rows, :].astype(F32)
            + rsb[0, 1, rows, :].astype(F32)
        ).astype(BF16)

    send(zsnd, zrcv, p_s.at[12], p_r.at[12], to_zl)
    stage_wait(f3, f4, 2)
    walsh(4, f4, f5)
    stage_start(f5, f6, 3)
    p_onward(1, zl)
    stage_wait(f5, f6, 3)

    def local_walsh(block):
        for m in range(COS):
            uu[m] = jnp.dot(block(m), hw[...], preferred_element_type=F32)

    local_walsh(lambda m: f6[:, :, 128 * m:128 * m + 128].reshape(ROWS, WALSH))
    me = 2 * x + zl

    @pl.loop(0, 8)
    def _(i):
        rows = pl.ds(pl.multiple_of(i * 16, 16), 16)
        u = [uu[m, rows, :] for m in range(COS)]
        ev = [u[m] + u[13 - m] for m in range(7)]
        od = [u[m] - u[13 - m] for m in range(7)]
        for n in range(COS):
            part = od if n % 2 else ev
            acc = part[0] * float(COSINE[0, n])
            for m in range(1, 7):
                acc = acc + part[m] * float(COSINE[m, n])
            rot[c, me, rows, 128 * n:128 * n + 128] = acc.astype(BF16)

    def rblk(h, xx, zz, cc):
        return rot.at[cc, 2 * xx + zz, pl.ds(WR * h, WR)]

    def to_sibling(h, n, xx, zz):
        b = rblk(h, xx, zz, c)
        send(b, b, k_s.at[15 * h + 7 + n], k_r.at[15 * h + 7 + n], to_co)

    def gather(h, n, xx, zz, dev):
        b = rblk(h, xx, zz, c)
        send(b, b, k_s.at[15 * h + n], k_r.at[15 * h + n], dev)

    def gathered(h, n, xx, zz, dev):
        arrived(rblk(h, xx, zz, c), k_s.at[15 * h + n], k_r.at[15 * h + n], dev)

    def gather_zl(h):
        gather(h, 0, x, zl, to_zl)
        to_sibling(h, 0, x, zl)

    def gather_own(h):
        gather(h, 1, x, zl, to_xp)
        gather(h, 4, x, zl, to_xm)

    def gather_partner(h):
        gathered(h, 0, x, zo, to_zl)
        gather(h, 2, x, zo, to_xp)
        gather(h, 5, x, zo, to_xm)
        to_sibling(h, 1, x, zo)

    def gather_on(h):
        gathered(h, 1, xm, zl, to_xm)
        gather(h, 3, xm, zl, to_xp)
        to_sibling(h, 2, xm, zl)
        gathered(h, 4, xp, zl, to_xp)
        to_sibling(h, 3, xp, zl)
        gathered(h, 5, xp, zo, to_xp)
        gather(h, 6, xp, zo, to_xm)
        to_sibling(h, 4, xp, zo)
        gathered(h, 2, xm, zo, to_xm)
        to_sibling(h, 5, xm, zo)

    def gather_end(h):
        gathered(h, 3, xo, zl, to_xm)
        to_sibling(h, 6, xo, zl)
        gathered(h, 6, xo, zo, to_xp)
        to_sibling(h, 7, xo, zo)
        for n, (xx, zz) in enumerate(
            ((x, zl), (x, zo), (xm, zl), (xp, zl), (xp, zo), (xm, zo), (xo, zl), (xo, zo))
        ):
            arrived(rblk(h, xx, zz, co), k_s.at[15 * h + 7 + n], k_r.at[15 * h + 7 + n], to_co)

    gather_zl(0)
    gather_zl(1)
    gather_zl(2)
    gather_zl(3)
    gather_own(0)
    gather_own(1)

    def rotate_back():
        p_arrived(1)
        arrived(zrcv, p_s.at[12], p_r.at[12], to_zl)

        @pl.loop(0, 8)
        def _(i):
            rows = pl.ds(pl.multiple_of(i * 16, 16), 16)
            s = (
                pbuf[0, zl, rows, :].astype(F32)
                + rsb[1, 0, rows, :].astype(F32)
                + rsb[1, 1, rows, :].astype(F32)
                + zrcv[rows, :].astype(F32)
            ).astype(BF16)
            hb[2 * i] = s[:, :HALF]
            hb[2 * i + 1] = s[:, HALF:]

        a2a_start(hb, r3, 0)

    def project(h):
        @pl.loop(0, 2)
        def _(par):
            a = rot[par, :, WR * h:WR * h + WR].reshape(8 * WR, WIDTH)
            for n in range(2):
                cols = slice(n * 256, n * 256 + 256)
                p = jnp.dot(a, wq[c, :, cols], preferred_element_type=F32)
                lo[h, :, par, :, :, cols] = p.astype(BF16).reshape(4, 2, WR, 256)

    def out_y(h):
        project(h)
        for j in range(1, 4):
            n = 6 * h + j - 1
            d = (y + j) % 4
            send(lo.at[h, d], tb.at[h, j - 1], t_s.at[n], t_r.at[n], (dp, d * 4 + zh))

    def out_z(h):
        for j in range(1, 4):
            n = 6 * h + j - 1
            arrived(tb.at[h, j - 1], t_s.at[n], t_r.at[n], (dp, (y + 4 - j) % 4 * 4 + zh))
        for par in range(2):
            total = lo[h, y, par].astype(F32)
            for j in range(3):
                total = total + tb[h, j, par].astype(F32)
            lz[h, par] = total.astype(BF16)
        for j in range(1, 4):
            n = 6 * h + j + 2
            d = (zh + j) % 4
            send(lz.at[h, d % 2, d // 2], td.at[h, j - 1], t_s.at[n], t_r.at[n], (dp, y * 4 + d))

    def out_end(h):
        total = lz[h, zh % 2, zh // 2].astype(F32)
        for j in range(1, 4):
            n = 6 * h + j + 2
            arrived(td.at[h, j - 1], t_s.at[n], t_r.at[n], (dp, y * 4 + (zh + 4 - j) % 4))
            total = total + td[h, j - 1].astype(F32)
        lov[WR * h:WR * h + WR, :] = total.astype(BF16)

    def down(half, lo_n, hi_n):
        @pl.loop(lo_n, hi_n)
        def _(n):
            cols = pl.ds(pl.multiple_of(n * 256, 256), 256)
            acc = None
            for par in range(2):
                a = rot[par, :, 64 * half:64 * half + 64, cols].reshape(512, 256)
                p = tn(a, gall[c, par, :, 64 * half:64 * half + 64].reshape(512, FEAT))
                acc = p if acc is None else acc + p
            gdv[cols, :] = acc if half == 0 else (gdv[cols, :] + acc) * dsq[cols, :]

    stores = []

    def store(src, dst):
        d = pltpu.make_async_copy(src, dst, o_s.at[len(stores)])
        d.start()
        stores.append(d)

    rotate_back()
    gather_partner(0)
    gather_on(0)
    gather_own(2)
    gather_partner(1)
    gather_end(0)
    out_y(0)
    gather_on(1)
    gather_own(3)
    gather_partner(2)
    a2a_wait(hb, r3, 0)
    walsh(16, r3, s4)
    a2a_start(s4, r4, 1)
    gather_end(1)
    out_y(1)
    gather_on(2)
    gather_partner(3)
    gather_end(2)
    out_y(2)
    out_z(0)
    gather_on(3)
    out_z(1)
    down(0, 0, 4)
    gather_end(3)
    out_y(3)
    out_z(2)
    down(0, 4, 7)
    down(1, 0, 4)
    store(gdv.at[pl.ds(0, 1024)], gd_out.at[pl.ds(0, 1024)])
    out_z(3)
    down(1, 4, 7)
    store(gdv.at[pl.ds(1024, 768)], gd_out.at[pl.ds(1024, 768)])
    a2a_wait(s4, r4, 1)

    def block_of(m):
        j, k = m // 7, m % 7
        return jnp.concatenate([r4[2 * i + j, :, 128 * k:128 * k + 128] for i in range(8)], axis=0)

    local_walsh(block_of)

    @pl.loop(0, 8)
    def _(i):
        rows = pl.ds(pl.multiple_of(i * 16, 16), 16)
        for m in range(7):
            evn = uu[0, rows, :] * float(COSINE[m, 0])
            odd = uu[1, rows, :] * float(COSINE[m, 1])
            for n in range(2, COS, 2):
                evn = evn + uu[n, rows, :] * float(COSINE[m, n])
                odd = odd + uu[n + 1, rows, :] * float(COSINE[m, n + 1])
            for mm, val in ((m, evn + odd), (13 - m, evn - odd)):
                cols = slice(128 * mm, 128 * mm + 128)
                gh = val * sign[:, cols]
                v = gate[rows, cols].astype(F32)
                sigma = jax.nn.sigmoid(v)
                ggv[rows, cols] = (
                    gh * up[rows, cols].astype(F32) * sigma * (1.0 + v * (1.0 - sigma))
                ).astype(BF16)
                guv[rows, cols] = (gh * (v * sigma)).astype(BF16)

    store(ggv, gg_out)
    store(guv, gu_out)
    for h in range(WAVES):
        out_end(h)
    store(lov, lo_out)
    for d in sent:
        d.wait_send()
    for d in stores:
        d.wait()


def finish(lo_i, gd_i, gg_i, gu_i, lo_o, gd_o, gg_o, gu_o, lo_v, gd_v, gg_v, gu_v, sem_i, sem_o):
    pieces = []
    for n in range(7):
        rows = pl.ds(256 * n, 256)
        pieces.append((gd_i.at[rows], gd_v.at[rows], gd_o.at[rows]))
    pieces += [(gg_i, gg_v, gg_o), (gu_i, gu_v, gu_o), (lo_i, lo_v, lo_o)]
    loads = [pltpu.make_async_copy(a, b, sem_i.at[n]) for n, (a, b, _) in enumerate(pieces)]
    stores = [pltpu.make_async_copy(b, o, sem_o.at[n]) for n, (_, b, o) in enumerate(pieces)]
    for d in loads:
        d.start()
    for d, e in zip(loads, stores):
        d.wait()
        e.start()
    for e in stores:
        e.wait()


def on_device(gate_pre, up_pre, down_rotated, exponents, signs, out_grad):
    anywhere = pl.BlockSpec(memory_space=pl.ANY)
    blocks = pltpu.VMEM((16, 16, HALF), BF16)
    dma = pltpu.SemaphoreType.DMA
    out_shape = (
        jax.ShapeDtypeStruct((ROWS, FEAT), BF16),
        jax.ShapeDtypeStruct((WIDTH, FEAT), F32),
        jax.ShapeDtypeStruct((ROWS, WIDTH), BF16),
        jax.ShapeDtypeStruct((ROWS, WIDTH), BF16),
    )
    outs = pl.pallas_call(
        kernel,
        out_shape=out_shape,
        in_specs=[anywhere] * 7,
        out_specs=(anywhere,) * 4,
        scratch_shapes=[
            pltpu.VMEM((ROWS, WIDTH), BF16),
            pltpu.VMEM((ROWS, WIDTH), BF16),
            pltpu.VMEM((WIDTH, FEAT), BF16),
            pltpu.VMEM((COS, FEAT), jnp.int32),
            pltpu.VMEM((WIDTH,), jnp.int32),
            pltpu.VMEM((WALSH, WALSH), BF16),
        ]
        + [pltpu.VMEM((4, 32, WIDTH), BF16)] * 7
        + [blocks] * 4
        + [
            pltpu.VMEM((COS, ROWS, WALSH), F32),
            pltpu.VMEM((2, 2, 8, ROWS, FEAT), BF16),
            pltpu.VMEM((2, WIDTH, FEAT), BF16),
            pltpu.VMEM((WIDTH, FEAT), F32),
            pltpu.VMEM((2, 8, ROWS, WIDTH), BF16),
            pltpu.VMEM((4, 2, ROWS, WIDTH), BF16),
            pltpu.VMEM((2, 2, 64, WIDTH), BF16),
            pltpu.VMEM((2, 2, ROWS, WIDTH), BF16),
            pltpu.VMEM((ROWS, WIDTH), BF16),
            pltpu.VMEM((ROWS, WIDTH), BF16),
            pltpu.VMEM((WAVES, 4, 2, 2, WR, FEAT), BF16),
            pltpu.VMEM((WAVES, 3, 2, 2, WR, FEAT), BF16),
            pltpu.VMEM((WAVES, 2, 2, WR, FEAT), BF16),
            pltpu.VMEM((WAVES, 3, WR, FEAT), BF16),
            pltpu.VMEM((ROWS, FEAT), BF16),
            pltpu.VMEM((WIDTH, FEAT), F32),
            pltpu.VMEM((ROWS, WIDTH), BF16),
            pltpu.VMEM((ROWS, WIDTH), BF16),
            dma((7,)), dma((5,)),
            dma((4, 4)), dma((4, 4)),
            dma((2, 16)), dma((2, 16)),
            dma((30,)), dma((30,)),
            dma((5,)), dma((5,)),
            dma((13,)), dma((13,)),
            dma((15 * WAVES,)), dma((15 * WAVES,)),
            dma((6 * WAVES,)), dma((6 * WAVES,)),
        ],
        compiler_params=pltpu.CompilerParams(
            collective_id=0, has_side_effects=True, vmem_limit_bytes=60 * 1024 * 1024
        ),
        cost_estimate=pl.CostEstimate(
            flops=11_300_000_000, bytes_accessed=9_000_000, transcendentals=2_000_000
        ),
    )(
        gate_pre, up_pre, down_rotated, exponents, signs, out_grad,
        jnp.asarray(walsh_signs(WALSH)),
    )
    return pl.pallas_call(
        finish,
        out_shape=out_shape,
        in_specs=[anywhere] * 4,
        out_specs=(anywhere,) * 4,
        scratch_shapes=[pltpu.VMEM(o.shape, o.dtype) for o in out_shape] + [dma((10,)), dma((10,))],
        compiler_params=pltpu.CompilerParams(vmem_limit_bytes=60 * 1024 * 1024),
    )(*outs)


def solution(mesh):
    return jax.shard_map(
        on_device,
        mesh=mesh,
        in_specs=(
            P("dp", "tensor"),
            P("dp", "tensor"),
            P("tensor", "dp"),
            P("tensor", "dp"),
            P("tensor"),
            P("tensor", "dp"),
        ),
        out_specs=(P("tensor", "dp"), P("tensor", "dp"), P("dp", "tensor"), P("dp", "tensor")),
        check_vma=False,
    )
```

```python
import jax
import jax.numpy as jnp
import ml_dtypes
import numpy as np
from jax import lax
from jax.experimental import pallas as pl
from jax.experimental.pallas import tpu as pltpu
from jax.sharding import PartitionSpec as P

ROWS = 128
WIDTH = 1792
FEAT = 512
WALSH = 128
COS = 14
HALF = 896
WAVES = 4
WR = ROWS // WAVES
F32 = jnp.float32
BF16 = jnp.bfloat16
MESH = pl.DeviceIdType.MESH

COSINE = np.sqrt(2.0 / COS) * np.cos(
    np.pi * (2 * np.arange(COS)[:, None] + 1) * np.arange(COS)[None, :] / (2.0 * COS)
)
COSINE[:, 0] = np.sqrt(1.0 / COS)
COSINE = COSINE / np.sqrt(WALSH)


def walsh_signs(order):
    a = np.arange(order)[:, None] & np.arange(order)[None, :]
    parity = np.zeros((order, order), np.int64)
    for bit in range(order.bit_length()):
        parity = parity + (a >> bit & 1)
    return (1.0 - 2.0 * (parity % 2)).astype(ml_dtypes.bfloat16)


def walsh(order, src, dst):
    scale = 1.0 / np.sqrt(order)
    height, width = src.shape[1:]

    @pl.loop(0, height // 16)
    def _(i):
        rows = pl.ds(pl.multiple_of(i * 16, 16), 16)

        @pl.loop(0, width // 128)
        def _(ch):
            cols = pl.ds(pl.multiple_of(ch * 128, 128), 128)
            v = [src[k, rows, cols].astype(F32) for k in range(order)]
            step = 1
            while step < order:
                w = list(v)
                for k in range(order):
                    if not k & step:
                        w[k] = v[k] + v[k + step]
                        w[k + step] = v[k] - v[k + step]
                v = w
                step *= 2
            for k in range(order):
                dst[k, rows, cols] = (v[k] * scale).astype(BF16)


def nt(a, b):
    return lax.dot_general(a, b, (((1,), (1,)), ((), ())), preferred_element_type=F32)


def tn(a, b):
    return lax.dot_general(a, b, (((0,), (0,)), ((), ())), preferred_element_type=F32)


def kernel(
    gate_h, up_h, w_h, ex_h, sg_h, g_h, hw_h,
    lo_out, gd_out, gg_out, gu_out,
    gate, up, w, ex, sg, hw,
    f0, f1, f2, f3, f4, f5, f6, hb, r3, s4, r4, uu,
    gall, wq, dsq, rot,
    pbuf, rsa, rsb, zsnd, zrcv,
    lo, tb, lz, td,
    lov, gdv, ggv, guv,
    i_s, o_s, f_s, f_r, a_s, a_r, g_s, g_r, c_s, c_r, p_s, p_r, k_s, k_r, t_s, t_r,
):
    dp = lax.axis_index("dp")
    t = lax.axis_index("tensor")
    x, zl, c = dp // 4, (dp // 2) % 2, dp % 2
    y, zh = t // 4, t % 4
    xp, xm, xo = (x + 1) % 4, (x + 3) % 4, (x + 2) % 4
    yp, ym, yo = (y + 1) % 4, (y + 3) % 4, (y + 2) % 4
    hp, hm, ho = (zh + 1) % 4, (zh + 3) % 4, (zh + 2) % 4
    zo, co = 1 - zl, 1 - c
    to_xp = (xp * 4 + zl * 2 + c, t)
    to_xm = (xm * 4 + zl * 2 + c, t)
    to_zl = (x * 4 + zo * 2 + c, t)
    to_co = (x * 4 + zl * 2 + co, t)
    to_yp, to_ym = (dp, yp * 4 + zh), (dp, ym * 4 + zh)
    to_hp, to_hm = (dp, y * 4 + hp), (dp, y * 4 + hm)

    def copy(src, dst, ss, rs, dev):
        return pltpu.make_async_remote_copy(
            src_ref=src, dst_ref=dst, send_sem=ss, recv_sem=rs, device_id=dev, device_id_type=MESH
        )

    sent = []

    def send(src, dst, ss, rs, dev):
        d = copy(src, dst, ss, rs, dev)
        d.start()
        sent.append(d)

    def arrived(dst, ss, rs, dev):
        copy(dst, dst, ss, rs, dev).wait_recv()

    g_in = pltpu.make_async_copy(g_h, gall.at[c, zh % 2, y * 2 + zh // 2], i_s.at[0])
    g_in.start()
    loads = [
        pltpu.make_async_copy(src, dst, i_s.at[1 + n])
        for n, (src, dst) in enumerate(((sg_h, sg), (gate_h, gate), (up_h, up), (ex_h, ex), (w_h, w), (hw_h, hw)))
    ]
    barrier = pltpu.get_barrier_semaphore()

    @pl.loop(1, 16)
    def _(j):
        pl.semaphore_signal(barrier, inc=1, device_id=(dp, (t + j) % 16), device_id_type=MESH)

    for dev in (to_xp, to_xm, to_zl, to_co):
        pl.semaphore_signal(barrier, inc=1, device_id=dev, device_id_type=MESH)
    for d in loads:
        d.start()
    g_in.wait()
    pl.semaphore_wait(barrier, 19)

    def gblk(core, yy, hh):
        return gall.at[core, hh % 2, yy * 2 + hh // 2]

    def ghalf(core, yy, hh, top):
        return gall.at[core, hh % 2, yy * 2 + hh // 2, pl.ds(0 if top else 64, 64)]

    zs = (zh, hm, hp, ho)

    def g_z(n, hh, top, dev):
        b = ghalf(c, y, hh, top)
        send(b, b, g_s.at[n], g_r.at[n], dev)

    def g_zd(n, hh, top, dev):
        arrived(ghalf(c, y, hh, top), g_s.at[n], g_r.at[n], dev)

    def g_y1(j, top):
        n = 6 + 6 * j + (0 if top else 2)
        b = ghalf(c, y, zs[j], top)
        send(b, b, g_s.at[n], g_r.at[n], to_yp)
        send(b, b, g_s.at[n + 1], g_r.at[n + 1], to_ym)

    def g_yd(j, n, yy, top, dev):
        n = 6 + 6 * j + n
        arrived(ghalf(c, yy, zs[j], top), g_s.at[n], g_r.at[n], dev)

    def g_y2(j):
        n = 6 + 6 * j
        g_yd(j, 0, ym, True, to_ym)
        b = ghalf(c, ym, zs[j], True)
        send(b, b, g_s.at[n + 4], g_r.at[n + 4], to_yp)
        g_yd(j, 3, yp, False, to_yp)
        b = ghalf(c, yp, zs[j], False)
        send(b, b, g_s.at[n + 5], g_r.at[n + 5], to_ym)

    def g_core(n, yy):
        b = gall.at[c, co, pl.ds(2 * yy, 2)]
        send(b, b, c_s.at[1 + n], c_r.at[1 + n], to_co)

    def g_cored(n, yy):
        arrived(gall.at[co, c, pl.ds(2 * yy, 2)], c_s.at[1 + n], c_r.at[1 + n], to_co)

    g_z(0, zh, True, to_hp)
    g_z(1, zh, False, to_hm)
    g_y1(0, True)
    g_y1(0, False)
    g_z(2, zh, False, to_hp)
    g_z(3, zh, True, to_hm)

    for d in loads[:3]:
        d.wait()
    sign = jnp.concatenate([sg[pl.ds(128 * m, 128)].reshape(1, 128) for m in range(COS)], axis=1)
    sign = 2.0 * sign.astype(F32) - 1.0

    @pl.loop(0, 8)
    def _(i):
        rows = pl.ds(pl.multiple_of(i * 16, 16), 16)
        v = gate[rows, :].astype(F32)
        h = (v * jax.nn.sigmoid(v) * up[rows, :].astype(F32)).astype(BF16).astype(F32)
        f0[i // 2, pl.ds(pl.multiple_of(i % 2 * 16, 16), 16), :] = (h * sign).astype(BF16)

    def stage_dev(n, d):
        return (dp, y * 4 + d) if n < 2 else (dp, d * 4 + zh)

    def stage_start(src, dst, n):
        me = zh if n < 2 else y
        for j in range(1, 4):
            d = (me + j) % 4
            copy(src.at[d], dst.at[me], f_s.at[n, j], f_r.at[n, j], stage_dev(n, d)).start()

    def stage_wait(src, dst, n):
        me = zh if n < 2 else y
        dst[me] = src[me]
        for j in range(1, 4):
            d = (me + 4 - j) % 4
            copy(src.at[d], dst.at[d], f_s.at[n, j], f_r.at[n, j], stage_dev(n, d)).wait()

    g_zd(0, hm, True, to_hm)
    g_z(4, hm, True, to_hp)
    g_y1(1, True)
    g_zd(1, hp, False, to_hp)
    g_z(5, hp, False, to_hm)
    g_y1(2, False)
    g_y2(0)
    g_zd(2, hm, False, to_hm)
    g_y1(1, False)
    g_zd(3, hp, True, to_hp)
    g_y1(2, True)
    stage_start(f0, f1, 0)

    for d in loads[3:]:
        d.wait()

    @pl.loop(0, 14)
    def _(i):
        scale = 7.0 * jnp.exp2(ex[pl.ds(i, 1), :].astype(F32))
        inv = 1.0 / scale
        for half in range(2):
            rows = pl.ds(pl.multiple_of(i * 128 + half * 64, 64), 64)
            s = jnp.tanh(w[rows, :].astype(F32) * inv)
            wq[c, rows, :] = (scale * s).astype(BF16)
            dsq[rows, :] = 1.0 - s * s

    send(wq.at[c], wq.at[c], c_s.at[0], c_r.at[0], to_co)

    g_zd(4, ho, True, to_hm)
    g_y1(3, True)
    g_zd(5, ho, False, to_hp)
    g_y1(3, False)
    g_core(0, y)
    g_y2(1)
    g_y2(2)

    def a2a_start(src, dst, n):
        @pl.loop(1, 16)
        def _(j):
            d = (t + j) % 16
            copy(src.at[d], dst.at[t], a_s.at[n, j], a_r.at[n, j], (dp, d)).start()

    def a2a_wait(src, dst, n):
        dst[t] = src[t]

        @pl.loop(1, 16)
        def _(j):
            d = (t + 16 - j) % 16
            copy(src.at[d], dst.at[d], a_s.at[n, j], a_r.at[n, j], (dp, d)).wait()

    top, low = pl.ds(0, 64), pl.ds(64, 64)

    def add_into(slot, z, half, src):
        @pl.loop(0, 4)
        def _(i):
            here = pl.ds(pl.multiple_of(i * 16, 16), 16)
            rows = pl.ds(pl.multiple_of(half * 64 + i * 16, 16), 16)
            pbuf[slot, z, rows, :] = (
                pbuf[slot, z, rows, :].astype(F32) + src[here, :].astype(F32)
            ).astype(BF16)

    def p_copy(k, n, src, dst, dev):
        return copy(src, dst, p_s.at[6 * k + n], p_r.at[6 * k + n], dev)

    p_far, p_next, p_last = [], [], []
    for k, z in ((0, zo), (1, zl)):
        p_far.append(p_copy(k, 0, pbuf.at[2, z, top], rsa.at[k, 0], to_xp))
        p_far.append(p_copy(k, 1, pbuf.at[2, z, low], rsa.at[k, 1], to_xm))
        p_next.append(p_copy(k, 2, pbuf.at[1, z, low], rsb.at[k, 0, low], to_xp))
        p_last.append(p_copy(k, 3, pbuf.at[3, z, top], rsb.at[k, 1, top], to_xm))
    sent.extend((*p_far, *p_next, *p_last))

    def p_onward(k, z):
        p_copy(k, 0, rsa.at[k, 0], rsa.at[k, 0], to_xm).wait_recv()
        add_into(1, z, 0, rsa.at[k, 0])
        d = p_copy(k, 4, pbuf.at[1, z, top], rsb.at[k, 0, top], to_xp)
        d.start()
        sent.append(d)
        p_copy(k, 1, rsa.at[k, 1], rsa.at[k, 1], to_xp).wait_recv()
        add_into(3, z, 1, rsa.at[k, 1])
        d = p_copy(k, 5, pbuf.at[3, z, low], rsb.at[k, 1, low], to_xm)
        d.start()
        sent.append(d)

    def p_arrived(k):
        p_copy(k, 2, rsb.at[k, 0, low], rsb.at[k, 0, low], to_xm).wait_recv()
        p_copy(k, 3, rsb.at[k, 1, top], rsb.at[k, 1, top], to_xp).wait_recv()
        p_copy(k, 4, rsb.at[k, 0, top], rsb.at[k, 0, top], to_xm).wait_recv()
        p_copy(k, 5, rsb.at[k, 1, low], rsb.at[k, 1, low], to_xp).wait_recv()

    def partial(n, q):
        g_cored(n, q)
        slot = (q + 4 - x) % 4
        a0 = gall[0, c, pl.ds(2 * q, 2)].reshape(256, FEAT)
        a1 = gall[1, c, pl.ds(2 * q, 2)].reshape(256, FEAT)
        for n in range(7):
            cols = slice(n * 256, (n + 1) * 256)
            p = nt(a0, wq[0, cols, :]) + nt(a1, wq[1, cols, :])
            pbuf[slot, :, :, cols] = p.astype(BF16).reshape(2, ROWS, 256)

        @pl.when(slot == 2)
        def _():
            p_far[0].start()
            p_far[1].start()

        @pl.when(slot == 1)
        def _():
            p_next[0].start()

        @pl.when(slot == 3)
        def _():
            p_last[0].start()

    arrived(wq.at[co], c_s.at[0], c_r.at[0], to_co)
    partial(0, y)
    g_y2(3)
    for j in range(4):
        g_yd(j, 2, ym, False, to_ym)
        g_yd(j, 1, yp, True, to_yp)
    g_core(1, ym)
    g_core(2, yp)
    partial(1, ym)
    partial(2, yp)
    for j in range(4):
        g_yd(j, 4, yo, True, to_ym)
        g_yd(j, 5, yo, False, to_yp)
    g_core(3, yo)
    partial(3, yo)
    stage_wait(f0, f1, 0)
    walsh(4, f1, f2)
    stage_start(f2, f3, 1)
    stage_wait(f2, f3, 1)
    stage_start(f3, f4, 2)
    p_onward(0, zo)
    for d in (p_far[2], p_far[3], p_next[1], p_last[1]):
        d.start()

    p_arrived(0)

    @pl.loop(0, 8)
    def _(i):
        rows = pl.ds(pl.multiple_of(i * 16, 16), 16)
        zsnd[rows, :] = (
            pbuf[0, zo, rows, :].astype(F32)
            + rsb[0, 0, rows, :].astype(F32)
            + rsb[0, 1, rows, :].astype(F32)
        ).astype(BF16)

    send(zsnd, zrcv, p_s.at[12], p_r.at[12], to_zl)
    stage_wait(f3, f4, 2)
    walsh(4, f4, f5)
    stage_start(f5, f6, 3)
    p_onward(1, zl)
    stage_wait(f5, f6, 3)

    def local_walsh(block):
        for m in range(COS):
            uu[m] = jnp.dot(block(m), hw[...], preferred_element_type=F32)

    local_walsh(lambda m: f6[:, :, 128 * m:128 * m + 128].reshape(ROWS, WALSH))
    me = 2 * x + zl

    @pl.loop(0, 8)
    def _(i):
        rows = pl.ds(pl.multiple_of(i * 16, 16), 16)
        u = [uu[m, rows, :] for m in range(COS)]
        ev = [u[m] + u[13 - m] for m in range(7)]
        od = [u[m] - u[13 - m] for m in range(7)]
        for n in range(COS):
            part = od if n % 2 else ev
            acc = part[0] * float(COSINE[0, n])
            for m in range(1, 7):
                acc = acc + part[m] * float(COSINE[m, n])
            rot[c, me, rows, 128 * n:128 * n + 128] = acc.astype(BF16)

    def rblk(h, xx, zz, cc):
        return rot.at[cc, 2 * xx + zz, pl.ds(WR * h, WR)]

    def to_sibling(h, n, xx, zz):
        b = rblk(h, xx, zz, c)
        send(b, b, k_s.at[15 * h + 7 + n], k_r.at[15 * h + 7 + n], to_co)

    def gather(h, n, xx, zz, dev):
        b = rblk(h, xx, zz, c)
        send(b, b, k_s.at[15 * h + n], k_r.at[15 * h + n], dev)

    def gathered(h, n, xx, zz, dev):
        arrived(rblk(h, xx, zz, c), k_s.at[15 * h + n], k_r.at[15 * h + n], dev)

    def gather_zl(h):
        gather(h, 0, x, zl, to_zl)
        to_sibling(h, 0, x, zl)

    def gather_own(h):
        gather(h, 1, x, zl, to_xp)
        gather(h, 4, x, zl, to_xm)

    def gather_partner(h):
        gathered(h, 0, x, zo, to_zl)
        gather(h, 2, x, zo, to_xp)
        gather(h, 5, x, zo, to_xm)
        to_sibling(h, 1, x, zo)

    def gather_on(h):
        gathered(h, 1, xm, zl, to_xm)
        gather(h, 3, xm, zl, to_xp)
        to_sibling(h, 2, xm, zl)
        gathered(h, 4, xp, zl, to_xp)
        to_sibling(h, 3, xp, zl)
        gathered(h, 5, xp, zo, to_xp)
        gather(h, 6, xp, zo, to_xm)
        to_sibling(h, 4, xp, zo)
        gathered(h, 2, xm, zo, to_xm)
        to_sibling(h, 5, xm, zo)

    def gather_end(h):
        gathered(h, 3, xo, zl, to_xm)
        to_sibling(h, 6, xo, zl)
        gathered(h, 6, xo, zo, to_xp)
        to_sibling(h, 7, xo, zo)
        for n, (xx, zz) in enumerate(
            ((x, zl), (x, zo), (xm, zl), (xp, zl), (xp, zo), (xm, zo), (xo, zl), (xo, zo))
        ):
            arrived(rblk(h, xx, zz, co), k_s.at[15 * h + 7 + n], k_r.at[15 * h + 7 + n], to_co)

    gather_zl(0)
    gather_zl(1)
    gather_zl(2)
    gather_zl(3)
    gather_own(0)
    gather_own(1)

    def rotate_back():
        p_arrived(1)
        arrived(zrcv, p_s.at[12], p_r.at[12], to_zl)

        @pl.loop(0, 8)
        def _(i):
            rows = pl.ds(pl.multiple_of(i * 16, 16), 16)
            s = (
                pbuf[0, zl, rows, :].astype(F32)
                + rsb[1, 0, rows, :].astype(F32)
                + rsb[1, 1, rows, :].astype(F32)
                + zrcv[rows, :].astype(F32)
            ).astype(BF16)
            hb[2 * i] = s[:, :HALF]
            hb[2 * i + 1] = s[:, HALF:]

        a2a_start(hb, r3, 0)

    def project(h):
        @pl.loop(0, 2)
        def _(par):
            a = rot[par, :, WR * h:WR * h + WR].reshape(8 * WR, WIDTH)
            for n in range(2):
                cols = slice(n * 256, n * 256 + 256)
                p = jnp.dot(a, wq[c, :, cols], preferred_element_type=F32)
                lo[h, :, par, :, :, cols] = p.astype(BF16).reshape(4, 2, WR, 256)

    def out_y(h):
        project(h)
        for j in range(1, 4):
            n = 6 * h + j - 1
            d = (y + j) % 4
            send(lo.at[h, d], tb.at[h, j - 1], t_s.at[n], t_r.at[n], (dp, d * 4 + zh))

    def out_z(h):
        for j in range(1, 4):
            n = 6 * h + j - 1
            arrived(tb.at[h, j - 1], t_s.at[n], t_r.at[n], (dp, (y + 4 - j) % 4 * 4 + zh))
        for par in range(2):
            total = lo[h, y, par].astype(F32)
            for j in range(3):
                total = total + tb[h, j, par].astype(F32)
            lz[h, par] = total.astype(BF16)
        for j in range(1, 4):
            n = 6 * h + j + 2
            d = (zh + j) % 4
            send(lz.at[h, d % 2, d // 2], td.at[h, j - 1], t_s.at[n], t_r.at[n], (dp, y * 4 + d))

    def out_end(h):
        total = lz[h, zh % 2, zh // 2].astype(F32)
        for j in range(1, 4):
            n = 6 * h + j + 2
            arrived(td.at[h, j - 1], t_s.at[n], t_r.at[n], (dp, y * 4 + (zh + 4 - j) % 4))
            total = total + td[h, j - 1].astype(F32)
        lov[WR * h:WR * h + WR, :] = total.astype(BF16)

    def down(half, lo_n, hi_n):
        @pl.loop(lo_n, hi_n)
        def _(n):
            cols = pl.ds(pl.multiple_of(n * 256, 256), 256)
            acc = None
            for par in range(2):
                a = rot[par, :, 64 * half:64 * half + 64, cols].reshape(512, 256)
                p = tn(a, gall[c, par, :, 64 * half:64 * half + 64].reshape(512, FEAT))
                acc = p if acc is None else acc + p
            gdv[cols, :] = acc if half == 0 else (gdv[cols, :] + acc) * dsq[cols, :]

    stores = []

    def store(src, dst):
        d = pltpu.make_async_copy(src, dst, o_s.at[len(stores)])
        d.start()
        stores.append(d)

    rotate_back()
    gather_partner(0)
    gather_on(0)
    gather_own(2)
    gather_partner(1)
    gather_end(0)
    out_y(0)
    gather_on(1)
    gather_own(3)
    gather_partner(2)
    a2a_wait(hb, r3, 0)
    walsh(16, r3, s4)
    a2a_start(s4, r4, 1)
    gather_end(1)
    out_y(1)
    gather_on(2)
    gather_partner(3)
    gather_end(2)
    out_y(2)
    out_z(0)
    gather_on(3)
    out_z(1)
    down(0, 0, 4)
    gather_end(3)
    out_y(3)
    out_z(2)
    down(0, 4, 7)
    down(1, 0, 4)
    store(gdv.at[pl.ds(0, 1024)], gd_out.at[pl.ds(0, 1024)])
    out_z(3)
    down(1, 4, 7)
    store(gdv.at[pl.ds(1024, 768)], gd_out.at[pl.ds(1024, 768)])
    a2a_wait(s4, r4, 1)

    def block_of(m):
        j, k = m // 7, m % 7
        return jnp.concatenate([r4[2 * i + j, :, 128 * k:128 * k + 128] for i in range(8)], axis=0)

    local_walsh(block_of)

    @pl.loop(0, 8)
    def _(i):
        rows = pl.ds(pl.multiple_of(i * 16, 16), 16)
        for m in range(7):
            evn = uu[0, rows, :] * float(COSINE[m, 0])
            odd = uu[1, rows, :] * float(COSINE[m, 1])
            for n in range(2, COS, 2):
                evn = evn + uu[n, rows, :] * float(COSINE[m, n])
                odd = odd + uu[n + 1, rows, :] * float(COSINE[m, n + 1])
            for mm, val in ((m, evn + odd), (13 - m, evn - odd)):
                cols = slice(128 * mm, 128 * mm + 128)
                gh = val * sign[:, cols]
                v = gate[rows, cols].astype(F32)
                sigma = jax.nn.sigmoid(v)
                ggv[rows, cols] = (
                    gh * up[rows, cols].astype(F32) * sigma * (1.0 + v * (1.0 - sigma))
                ).astype(BF16)
                guv[rows, cols] = (gh * (v * sigma)).astype(BF16)

    store(ggv, gg_out)
    store(guv, gu_out)
    for h in range(WAVES):
        out_end(h)
    store(lov, lo_out)
    for d in sent:
        d.wait_send()
    for d in stores:
        d.wait()


def finish(lo_i, gd_i, gg_i, gu_i, lo_o, gd_o, gg_o, gu_o, lo_v, gd_v, gg_v, gu_v, sem_i, sem_o):
    pieces = []
    for n in range(7):
        rows = pl.ds(256 * n, 256)
        pieces.append((gd_i.at[rows], gd_v.at[rows], gd_o.at[rows]))
    pieces += [(gg_i, gg_v, gg_o), (gu_i, gu_v, gu_o), (lo_i, lo_v, lo_o)]
    loads = [pltpu.make_async_copy(a, b, sem_i.at[n]) for n, (a, b, _) in enumerate(pieces)]
    stores = [pltpu.make_async_copy(b, o, sem_o.at[n]) for n, (_, b, o) in enumerate(pieces)]
    for d in loads:
        d.start()
    for d, e in zip(loads, stores):
        d.wait()
        e.start()
    for e in stores:
        e.wait()


def on_device(gate_pre, up_pre, down_rotated, exponents, signs, out_grad):
    anywhere = pl.BlockSpec(memory_space=pl.ANY)
    blocks = pltpu.VMEM((16, 16, HALF), BF16)
    dma = pltpu.SemaphoreType.DMA
    out_shape = (
        jax.ShapeDtypeStruct((ROWS, FEAT), BF16),
        jax.ShapeDtypeStruct((WIDTH, FEAT), F32),
        jax.ShapeDtypeStruct((ROWS, WIDTH), BF16),
        jax.ShapeDtypeStruct((ROWS, WIDTH), BF16),
    )
    outs = pl.pallas_call(
        kernel,
        out_shape=out_shape,
        in_specs=[anywhere] * 7,
        out_specs=(anywhere,) * 4,
        scratch_shapes=[
            pltpu.VMEM((ROWS, WIDTH), BF16),
            pltpu.VMEM((ROWS, WIDTH), BF16),
            pltpu.VMEM((WIDTH, FEAT), BF16),
            pltpu.VMEM((COS, FEAT), jnp.int32),
            pltpu.VMEM((WIDTH,), jnp.int32),
            pltpu.VMEM((WALSH, WALSH), BF16),
        ]
        + [pltpu.VMEM((4, 32, WIDTH), BF16)] * 7
        + [blocks] * 4
        + [
            pltpu.VMEM((COS, ROWS, WALSH), F32),
            pltpu.VMEM((2, 2, 8, ROWS, FEAT), BF16),
            pltpu.VMEM((2, WIDTH, FEAT), BF16),
            pltpu.VMEM((WIDTH, FEAT), F32),
            pltpu.VMEM((2, 8, ROWS, WIDTH), BF16),
            pltpu.VMEM((4, 2, ROWS, WIDTH), BF16),
            pltpu.VMEM((2, 2, 64, WIDTH), BF16),
            pltpu.VMEM((2, 2, ROWS, WIDTH), BF16),
            pltpu.VMEM((ROWS, WIDTH), BF16),
            pltpu.VMEM((ROWS, WIDTH), BF16),
            pltpu.VMEM((WAVES, 4, 2, 2, WR, FEAT), BF16),
            pltpu.VMEM((WAVES, 3, 2, 2, WR, FEAT), BF16),
            pltpu.VMEM((WAVES, 2, 2, WR, FEAT), BF16),
            pltpu.VMEM((WAVES, 3, WR, FEAT), BF16),
            pltpu.VMEM((ROWS, FEAT), BF16),
            pltpu.VMEM((WIDTH, FEAT), F32),
            pltpu.VMEM((ROWS, WIDTH), BF16),
            pltpu.VMEM((ROWS, WIDTH), BF16),
            dma((7,)), dma((5,)),
            dma((4, 4)), dma((4, 4)),
            dma((2, 16)), dma((2, 16)),
            dma((30,)), dma((30,)),
            dma((5,)), dma((5,)),
            dma((13,)), dma((13,)),
            dma((15 * WAVES,)), dma((15 * WAVES,)),
            dma((6 * WAVES,)), dma((6 * WAVES,)),
        ],
        compiler_params=pltpu.CompilerParams(
            collective_id=0, has_side_effects=True, vmem_limit_bytes=60 * 1024 * 1024
        ),
        cost_estimate=pl.CostEstimate(
            flops=11_300_000_000, bytes_accessed=9_000_000, transcendentals=2_000_000
        ),
    )(
        gate_pre, up_pre, down_rotated, exponents, signs, out_grad,
        jnp.asarray(walsh_signs(WALSH)),
    )
    return pl.pallas_call(
        finish,
        out_shape=out_shape,
        in_specs=[anywhere] * 4,
        out_specs=(anywhere,) * 4,
        scratch_shapes=[pltpu.VMEM(o.shape, o.dtype) for o in out_shape] + [dma((10,)), dma((10,))],
        compiler_params=pltpu.CompilerParams(vmem_limit_bytes=60 * 1024 * 1024),
    )(*outs)


def solution(mesh):
    return jax.shard_map(
        on_device,
        mesh=mesh,
        in_specs=(
            P("dp", "tensor"),
            P("dp", "tensor"),
            P("tensor", "dp"),
            P("tensor", "dp"),
            P("tensor"),
            P("tensor", "dp"),
        ),
        out_specs=(P("tensor", "dp"), P("tensor", "dp"), P("dp", "tensor"), P("dp", "tensor")),
        check_vma=False,
    )
```
